128 devices in a mesh: cand: 8 (over z_hi, y), tp: 16 (over x, z_lo, core).
Axes of the slice: x: 4, y: 4, z: 4 (z_hi: 2, z_lo: 2; z = z_hi * 2 + z_lo), core: 2. Of those that a mesh axis runs over, the one named last changes fastest.
Arguments:
- tokens: bfloat16 [512, 4096], P(None, 'cand'), may hold values from -6 to 6
- attn_gain: float32 [4096], P('cand'), may hold values from 0.5 to 1.5
- ffn_gain: float32 [4096], P('cand'), may hold values from 0.5 to 1.5
- w_query: bfloat16 [4096, 4096], P('cand', 'tp'), may hold values from -40 to 40
- w_key: bfloat16 [4096, 1024], P('cand'), may hold values from -1 to 1
- w_value: bfloat16 [4096, 1024], P('cand'), may hold values from -0.09375 to 0.09375
- w_out: bfloat16 [4096, 4096], P('tp', 'cand'), may hold values from -0.09375 to 0.09375
- w_gate: bfloat16 [4096, 14336], P('cand', 'tp'), may hold values from -0.09375 to 0.09375
- w_up: bfloat16 [4096, 14336], P('cand', 'tp'), may hold values from -0.09375 to 0.09375
- w_down: bfloat16 [14336, 4096], P('tp', 'cand'), may hold values from -0.046875 to 0.046875
- doc_ids: int32 [512], replicated, may hold values from 0 to 3, never falling along the last dimension, each value on 1 to 256 neighbouring positions
- widths: int32 [8], replicated, may hold values from 16 to 12288, as said below
Outputs:
- grad_gate: bfloat16 [8, 4096, 12288], P('cand', None, 'tp')
- grad_up: bfloat16 [8, 4096, 12288], P('cand', None, 'tp')
- grad_down: bfloat16 [8, 12288, 4096], P('cand', 'tp')
The draws below stay inside these ranges and needn't reach their ends.
Inputs may be any that keep to these rules, and one draw needn't show every extreme that they name: `widths`: each entry is a multiple of 16; some candidate keeps 12288 units.
All inputs are finite; a program needn't handle non-finite values.
Results may differ from the reference program's by a relative error of at most 0.035.
Values may be sent and summed in bfloat16 or wider, within the bound.
No kernel may reach another device: no remote copies, remote signals or barrier semaphores. Data moves between devices by JAX's collectives and lax.ppermute only.
A program may use at most 192 MiB of HBM per device.

```python
import math
import jax
import jax.numpy as jnp
import numpy as np
from jax import lax

D = 4096
HEADS = 32
KV_HEADS = 8
HEAD_DIM = 128
FF = 14336
CAND_DEV = 768
TOK = 512
CANDS = 8
CAND_WIDTH = 12288
N_TP = 16


def draw_w_key(key, part):
    key = jax.random.fold_in(key, 21)
    fresh_noise = jnp.clip(jax.random.normal(key, (D, KV_HEADS * HEAD_DIM), jnp.float32), -6.0, 6.0) * D ** (-0.5)
    return fresh_noise.astype(jnp.bfloat16)


def draw_w_query(key, part):
    key = jax.random.fold_in(key, 22)
    noise_key = jax.random.fold_in(key, 0)
    fresh_noise = jnp.clip(jax.random.normal(noise_key, (D, HEADS * HEAD_DIM), jnp.float32), -6.0, 6.0) * D ** (-0.5)
    return fresh_noise.astype(jnp.bfloat16)


def draw_widths(key, part):
    key = jax.random.fold_in(key, 5)
    slot_key, full_key = jax.random.split(key)
    slot_counts = jax.random.randint(slot_key, (CANDS,), max(1, CAND_DEV // 6), CAND_DEV + 1)
    widest = jax.random.randint(full_key, (), 0, CANDS)
    slot_counts = jnp.where(jnp.arange(CANDS) == widest, CAND_DEV, slot_counts)
    return (slot_counts * (CAND_WIDTH // CAND_DEV)).astype(jnp.int32)


def steps_of(key, extent, cuts, least, largest):
    factor_of = 1.0
    for dim, blocks in cuts:
        draws = jax.random.uniform(jax.random.fold_in(jax.random.fold_in(key, 6), dim), (blocks,), jnp.float32, least / len(cuts), largest / len(cuts))
        factor_of = factor_of * jnp.repeat(jnp.exp(draws), extent[dim] // blocks).reshape((-1,) + (1,) * (len(extent) - 1 - dim))
    return factor_of


def profile(amount, total, reach, skew):
    portions = [(1 << 20) // math.isqrt(rank ** skew) + 1 for rank in range(2, amount + 1)]
    rest, counts = total - reach - (amount - 1), [1] * (amount - 1)
    while rest > 0:
        free = [i for i in range(amount - 1) if counts[i] < reach]
        mass, remaining = sum([portions[i] for i in free]), rest
        for i in free:
            addition = min(reach - counts[i], max(1, remaining * portions[i] // mass), rest)
            counts[i] = counts[i] + addition
            rest = rest - addition
    return np.array([reach] + counts)


def uneven_parts(stream_key, number_of, total, most, lean):
    if number_of == 2:
        one = jax.random.randint(stream_key, (), max(1, total - most), min(most, total - 1) + 1)
        return jnp.stack([one, total - one])
    tallies = jnp.asarray(profile(number_of, total, most, lean), jnp.int32)
    pairs = (number_of - 1) // 2
    giver, sink = tallies[1:1 + 2 * pairs:2], tallies[2:2 + 2 * pairs:2]
    slack = jnp.minimum(giver - 1, most - sink)
    passed = jax.random.randint(jax.random.fold_in(stream_key, 1), (pairs,), 0, 1 << 20) % (slack + 1)
    tallies = tallies.at[1:1 + 2 * pairs:2].set(giver - passed).at[2:2 + 2 * pairs:2].set(sink + passed)
    return tallies[jax.random.permutation(jax.random.fold_in(stream_key, 2), number_of)]


def scatter_about(key, extent, spread, bound, cuts=(), held_as=jnp.bfloat16):
    values = jax.random.normal(key, extent, jnp.float32) * spread
    if len(cuts) > 0:
        values = steps_of(key, extent, cuts, -0.22, 0.18) * values
    return jnp.clip(values, min=-bound, max=bound).astype(held_as)


def setup_inputs(seed: int = 0) -> dict:
    keys = jax.random.split(jax.random.key(seed), 13)
    return {
        "tokens": scatter_about(keys[0], (TOK, D), 1.0, 6.0, ((1, 8),)),
        "attn_gain": jnp.clip(1.0 + 0.1 * jax.random.normal(keys[1], (D,), jnp.float32), 0.5, 1.5),
        "ffn_gain": jnp.clip(1.0 + 0.1 * jax.random.normal(keys[2], (D,), jnp.float32), 0.5, 1.5),
        "w_query": draw_w_query(jax.random.fold_in(keys[12], 71), 0),
        "w_key": draw_w_key(jax.random.fold_in(keys[12], 71), 0),
        "w_value": scatter_about(keys[5], (D, KV_HEADS * HEAD_DIM), D ** -0.5, 0.09375, ((0, 8),)),
        "w_out": scatter_about(keys[6], (HEADS * HEAD_DIM, D), (HEADS * HEAD_DIM) ** -0.5, 0.09375, ((0, 16), (1, 8))),
        "w_gate": scatter_about(keys[7], (D, FF), D ** -0.5, 0.09375, ((0, 8), (1, 16))),
        "w_up": scatter_about(keys[8], (D, FF), D ** -0.5, 0.09375, ((0, 8), (1, 16))),
        "w_down": scatter_about(keys[9], (FF, D), FF ** -0.5, 0.046875, ((0, 16), (1, 8))),
        "doc_ids": jnp.searchsorted(jnp.cumsum(uneven_parts(keys[10], 4, TOK, TOK // 2, 1)), jnp.arange(TOK), side="right").astype(jnp.int32),
        "widths": draw_widths(jax.random.fold_in(keys[12], 71), 0),
    }


EPSILON = 1e-05

def rms_normed(rows, gain):
    wide_rows = rows.astype(jnp.float32)
    row_scale = lax.rsqrt(lax.optimization_barrier(jnp.sum(wide_rows * wide_rows, axis=1)) / D + EPSILON)
    return (wide_rows * row_scale[:, None] * gain[None, :]).astype(jnp.bfloat16)

def pick_slots(array):
    per_dev = FF // N_TP
    return array.reshape(array.shape[0], N_TP, per_dev)[:, :, :CAND_DEV].reshape(array.shape[0], CAND_WIDTH)

def reference(tokens, attn_gain, ffn_gain, w_query, w_key, w_value, w_out, w_gate, w_up, w_down, doc_ids, widths):
    normed = rms_normed(tokens, attn_gain)
    group_size = HEADS // KV_HEADS
    query = jnp.dot(normed, w_query, preferred_element_type=jnp.float32).astype(jnp.bfloat16)
    key_rows = jnp.dot(normed, w_key, preferred_element_type=jnp.float32).astype(jnp.bfloat16)
    value_rows = jnp.dot(normed, w_value, preferred_element_type=jnp.float32).astype(jnp.bfloat16)
    query_four = query.astype(jnp.float32).reshape(TOK, KV_HEADS, group_size, HEAD_DIM)
    key_three = key_rows.astype(jnp.float32).reshape(TOK, KV_HEADS, HEAD_DIM)
    value_three = value_rows.astype(jnp.float32).reshape(TOK, KV_HEADS, HEAD_DIM)
    scores = jnp.einsum('qkgd,skd->kgqs', query_four, key_three) * HEAD_DIM ** (-0.5)
    position = jnp.arange(TOK, dtype=jnp.int32)
    allowed = (position[None, :] <= position[:, None]) & (doc_ids[None, :] == doc_ids[:, None])
    scores = jnp.where(allowed[None, None], scores, -1e+30)
    peak_score = lax.optimization_barrier(jnp.max(scores, axis=-1, keepdims=True))
    expo = jnp.exp(scores - peak_score)
    probs = (expo / lax.optimization_barrier(jnp.sum(expo, axis=-1, keepdims=True))).astype(jnp.bfloat16)
    attended = jnp.einsum('kgqs,skd->qkgd', probs.astype(jnp.float32), value_three)
    attended = attended.astype(jnp.bfloat16).reshape(TOK, HEADS * HEAD_DIM)
    residual = (tokens.astype(jnp.float32) + jnp.dot(attended, w_out, preferred_element_type=jnp.float32)).astype(jnp.bfloat16)
    ffn_in = rms_normed(residual, ffn_gain)
    gate_sum = jnp.dot(ffn_in, w_gate, preferred_element_type=jnp.float32)
    up_sum = jnp.dot(ffn_in, w_up, preferred_element_type=jnp.float32)
    sigmoid_gate = jax.nn.sigmoid(gate_sum)
    activated = gate_sum * sigmoid_gate
    hidden = (activated * up_sum).astype(jnp.bfloat16)
    target = jnp.dot(hidden, w_down, preferred_element_type=jnp.float32).astype(jnp.bfloat16)
    target_wide = target.astype(jnp.float32)
    gate_sel = pick_slots(gate_sum)
    up_sel = pick_slots(up_sum)
    sigmoid_sel = pick_slots(sigmoid_gate)
    activated_sel = pick_slots(activated)
    hidden_sel = pick_slots(hidden)
    down_sel = w_down.reshape(N_TP, FF // N_TP, D)[:, :CAND_DEV].reshape(CAND_WIDTH, D)
    slot_local = jnp.arange(CAND_WIDTH, dtype=jnp.int32) % CAND_DEV
    slope = sigmoid_sel * (1.0 + gate_sel * (1.0 - sigmoid_sel))

    def one_candidate(cand_width):
        keep_mask = (slot_local < cand_width // N_TP)[None, :]
        used_hidden = jnp.where(keep_mask, hidden_sel, jnp.zeros((), jnp.bfloat16))
        error_rows = jnp.dot(used_hidden, down_sel, preferred_element_type=jnp.float32) - target_wide
        grad_rows = error_rows.astype(jnp.bfloat16)
        back_sum = jnp.dot(grad_rows, down_sel.T, preferred_element_type=jnp.float32)
        gate_term = jnp.where(keep_mask, back_sum * up_sel * slope, 0.0).astype(jnp.bfloat16)
        up_term = jnp.where(keep_mask, back_sum * activated_sel, 0.0).astype(jnp.bfloat16)
        gate_grad = jnp.dot(ffn_in.T, gate_term, preferred_element_type=jnp.float32).astype(jnp.bfloat16)
        up_grad = jnp.dot(ffn_in.T, up_term, preferred_element_type=jnp.float32).astype(jnp.bfloat16)
        down_grad = jnp.dot(used_hidden.T, grad_rows, preferred_element_type=jnp.float32).astype(jnp.bfloat16)
        return (gate_grad, up_grad, down_grad)
    grad_gate, grad_up, grad_down = lax.map(one_candidate, widths)
    return (grad_gate, grad_up, grad_down)
```

```python
import jax
import jax.numpy as jnp
from jax import lax
from jax.sharding import PartitionSpec as P

D = 4096
HEADS = 32
KV_HEADS = 8
HEAD_DIM = 128
CAND_DEV = 768
LANES = 128
EPSILON = 1e-05
BF = jnp.bfloat16
F32 = jnp.float32

CORE_PAIRS = [(i, i ^ 1) for i in range(16)]
SAME_CORE = [list(range(core, 16, 2)) for core in range(2)]


def two_parts(column):
    high = lax.reduce_precision(column, 8, 7)
    low = column - high
    pad = jnp.zeros((column.shape[0], LANES - 2), BF)
    return jnp.concatenate([high.astype(BF)[:, None], low.astype(BF)[:, None], pad], axis=1)


def exchange(blocks, axis, groups=None):
    return lax.all_to_all(blocks, axis, 0, 0, axis_index_groups=groups)


def sum_scatter(blocks, axis, groups=None):
    return jnp.sum(exchange(blocks, axis, groups).astype(F32), axis=0)


def gather_blocks(block, axis, count, groups=None):
    return exchange(jnp.broadcast_to(block[None], (count,) + block.shape), axis, groups)


def shards(
    tokens,
    attn_gain,
    ffn_gain,
    w_query,
    w_key,
    w_value,
    w_out,
    w_gate,
    w_up,
    w_down,
    doc_ids,
    widths,
):
    cand_index = lax.axis_index("cand")
    tp_index = lax.axis_index("tp")
    core = tp_index % 2
    cands = lax.axis_size("cand")
    tps = lax.axis_size("tp")
    chips = tps // 2
    tok_count = tokens.shape[0]
    width = tokens.shape[1]
    ff_dev = w_gate.shape[1]
    tok_cand = tok_count // cands
    tok_tp = tok_count // tps
    tok_half = tok_cand // 2

    down_all = lax.all_gather(w_down, "cand", axis=0)

    wide_in = tokens.astype(F32)
    scaled_in = (wide_in * attn_gain[None, :]).astype(BF)
    heads_dev = w_query.shape[1] // HEAD_DIM
    group_size = HEADS // KV_HEADS
    kv_index = tp_index * heads_dev // group_size
    key_cols = lax.dynamic_slice_in_dim(w_key, kv_index * HEAD_DIM, HEAD_DIM, 1)
    value_cols = lax.dynamic_slice_in_dim(w_value, kv_index * HEAD_DIM, HEAD_DIM, 1)
    parts = [
        jnp.dot(scaled_in, cols, preferred_element_type=F32).astype(BF)
        for cols in (w_query, key_cols, value_cols)
    ]
    parts.append(two_parts(jnp.sum(wide_in * wide_in, axis=1)))
    part = jnp.concatenate(parts, axis=1)
    total = sum_scatter(part.reshape(cands, tok_cand, part.shape[1]), "cand")
    qkv_width = part.shape[1] - LANES
    squares = total[:, qkv_width] + total[:, qkv_width + 1]
    qkv_rows = (total[:, :qkv_width] * lax.rsqrt(squares / D + EPSILON)[:, None]).astype(BF)
    qkv = gather_blocks(qkv_rows, "cand", cands).reshape(tok_count, qkv_width)
    q_width = heads_dev * HEAD_DIM
    query = qkv[:, :q_width].reshape(tok_count, heads_dev, HEAD_DIM)
    key_rows = qkv[:, q_width : q_width + HEAD_DIM]
    value_rows = qkv[:, q_width + HEAD_DIM :]

    scores = jnp.einsum(
        "qhd,kd->hqk", query, key_rows, preferred_element_type=F32
    ) * HEAD_DIM ** (-0.5)
    position = lax.iota(jnp.int32, tok_count)
    allowed = (position[None, :] <= position[:, None]) & (doc_ids[None, :] == doc_ids[:, None])
    scores = jnp.where(allowed[None], scores, -1e30)
    peak_score = jnp.max(scores, axis=-1, keepdims=True)
    expo = jnp.exp(scores - peak_score)
    weights_bf = (expo / jnp.sum(expo, axis=-1, keepdims=True)).astype(BF)
    attended = jnp.einsum("hqk,kd->qhd", weights_bf, value_rows, preferred_element_type=F32)
    attended = attended.astype(BF).reshape(tok_count, heads_dev * HEAD_DIM)
    out_part = jnp.dot(attended, w_out, preferred_element_type=F32).astype(BF)
    attn_rows = sum_scatter(out_part.reshape(tps, tok_tp, width), "tp")
    own_rows = lax.dynamic_slice_in_dim(tokens, tp_index * tok_tp, tok_tp, 0)
    residual_rows = (own_rows.astype(F32) + attn_rows).astype(BF)
    residual = gather_blocks(residual_rows, "tp", tps).reshape(tok_count, width)

    wide_res = residual.astype(F32)
    scaled_res = (wide_res * ffn_gain[None, :]).astype(BF)
    parts = [
        jnp.dot(scaled_res, cols, preferred_element_type=F32).astype(BF) for cols in (w_gate, w_up)
    ]
    parts.append(two_parts(jnp.sum(wide_res * wide_res, axis=1)))
    part = jnp.concatenate(parts, axis=1)
    total = sum_scatter(part.reshape(cands, tok_cand, part.shape[1]), "cand")
    squares = total[:, 2 * ff_dev] + total[:, 2 * ff_dev + 1]
    row_scale = lax.rsqrt(squares / D + EPSILON)
    gate_own = total[:, :ff_dev] * row_scale[:, None]
    up_own = total[:, ff_dev : 2 * ff_dev] * row_scale[:, None]
    hidden_own = (gate_own * jax.nn.sigmoid(gate_own) * up_own).astype(BF)

    sums_own = jnp.concatenate(
        [gate_own[:, :CAND_DEV].astype(BF), up_own[:, :CAND_DEV].astype(BF), two_parts(row_scale)], axis=1
    )
    sums_all = lax.all_gather(sums_own, "cand", axis=0)
    res_half = lax.dynamic_slice_in_dim(
        scaled_res.reshape(cands, 2, tok_half, width), core, 1, 1
    ).reshape(cands * tok_half, width)
    res_first = lax.all_gather(res_half, "cand", axis=0)
    res_second = lax.ppermute(res_first, "tp", CORE_PAIRS)

    live = widths // tps
    dropped = lax.iota(jnp.int32, ff_dev)[None, None, :] >= live[:, None, None]

    def dropped_output(half):
        rows = lax.dynamic_slice_in_dim(hidden_own, half * tok_half, tok_half, 0)
        rows = jnp.where(dropped, -rows[None], jnp.zeros((), BF)).reshape(cands * tok_half, ff_dev)
        return jnp.einsum("ru,fuk->frk", rows, down_all, preferred_element_type=F32).astype(BF)

    away = lax.ppermute(dropped_output(1 - core), "tp", CORE_PAIRS)
    pair_sum = (dropped_output(core).astype(F32) + away.astype(F32)).astype(BF)
    error_block = sum_scatter(pair_sum, "tp", SAME_CORE).astype(BF)
    grad_block = exchange(error_block.reshape(cands, tok_half, width), "cand")
    grad_first = gather_blocks(grad_block.reshape(cands * tok_half, width), "tp", chips, SAME_CORE)
    grad_second = lax.ppermute(grad_first, "tp", CORE_PAIRS)

    cand_live = jnp.sum(jnp.where(lax.iota(jnp.int32, widths.shape[0]) == cand_index, live, 0))
    keep_mask = (lax.iota(jnp.int32, CAND_DEV) < cand_live)[None, :]
    down_sel = down_all[:, :CAND_DEV]

    def terms(half, grad):
        sums = lax.dynamic_slice_in_dim(
            sums_all.reshape(cands, 2, tok_half, sums_all.shape[2]), half, 1, 1
        ).reshape(cands * tok_half, sums_all.shape[2]).astype(F32)
        gate_sel = sums[:, :CAND_DEV]
        up_sel = sums[:, CAND_DEV : 2 * CAND_DEV]
        scale = sums[:, 2 * CAND_DEV : 2 * CAND_DEV + 1] + sums[:, 2 * CAND_DEV + 1 : 2 * CAND_DEV + 2]
        sigmoid_sel = jax.nn.sigmoid(gate_sel)
        activated = gate_sel * sigmoid_sel
        slope = sigmoid_sel * (1.0 + gate_sel * (1.0 - sigmoid_sel))
        used = jnp.where(keep_mask, activated * up_sel, 0.0).astype(BF)
        back = jnp.einsum("fnk,fuk->nu", grad, down_sel, preferred_element_type=F32) * scale
        gate_term = jnp.where(keep_mask, back * up_sel * slope, 0.0).astype(BF)
        up_term = jnp.where(keep_mask, back * activated, 0.0).astype(BF)
        return used, gate_term, up_term

    first = terms(core, grad_first)
    second = terms(1 - core, grad_second)
    used, gate_term, up_term = (jnp.concatenate(pair, axis=0) for pair in zip(first, second))
    res_all = jnp.concatenate([res_first, res_second], axis=1)
    grad_all = jnp.concatenate([grad_first, grad_second], axis=1)

    def features_by_slots(term):
        grad = jnp.einsum("fnd,nu->fdu", res_all, term, preferred_element_type=F32)
        return grad.astype(BF).reshape(1, D, CAND_DEV)

    down_grad = jnp.einsum("nu,fnd->ufd", used, grad_all, preferred_element_type=F32)
    down_grad = down_grad.astype(BF).reshape(1, CAND_DEV, D)
    return features_by_slots(gate_term), features_by_slots(up_term), down_grad


def solution(mesh):
    in_specs = (
        P(None, "cand"),
        P("cand"),
        P("cand"),
        P("cand", "tp"),
        P("cand", None),
        P("cand", None),
        P("tp", "cand"),
        P("cand", "tp"),
        P("cand", "tp"),
        P("tp", "cand"),
        P(),
        P(),
    )
    out_specs = (P("cand", None, "tp"), P("cand", None, "tp"), P("cand", "tp", None))
    return jax.shard_map(shards, mesh=mesh, in_specs=in_specs, out_specs=out_specs, check_vma=False)
```

```python
import functools

import jax
import jax.numpy as jnp
from jax import lax
from jax.experimental import pallas as pl
from jax.experimental.pallas import tpu as pltpu
from jax.sharding import PartitionSpec as P

D = 4096
HEADS = 32
KV_HEADS = 8
HEAD_DIM = 128
CAND_DEV = 768
LANES = 128
EPSILON = 1e-05
BF = jnp.bfloat16
F32 = jnp.float32

CORE_PAIRS = [(i, i ^ 1) for i in range(16)]
ACROSS_Z = [(i, i ^ 4) for i in range(8)]
SAME_Z = [[0, 1, 2, 3], [4, 5, 6, 7]]
SAME_CORE_ALL = [[c * 16 + t for c in range(8) for t in range(core, 16, 2)] for core in range(2)]
SAME_CORE = [list(range(core, 16, 2)) for core in range(2)]


def exchange(blocks, axis, groups=None):
    return lax.all_to_all(blocks, axis, 0, 0, axis_index_groups=groups)


def lanes_of(column):
    high = column.astype(BF).astype(F32)
    lane = lax.broadcasted_iota(jnp.int32, (column.shape[0], LANES), 1)
    return jnp.where(lane == 0, high, jnp.where(lane == 1, column - high, 0.0)).astype(BF)


def column_of(lanes):
    return lanes[:, 0:1].astype(F32) + lanes[:, 1:2].astype(F32)


def params(limit_mib):
    return pltpu.CompilerParams(
        dimension_semantics=("arbitrary",), vmem_limit_bytes=limit_mib << 20
    )


def cost(flops, bytes_accessed, transcendentals=0):
    return pl.CostEstimate(
        flops=flops, bytes_accessed=bytes_accessed, transcendentals=transcendentals
    )


def project_kernel(scalars, rows, gain, *refs):
    *weights, out, scaled_out = refs
    wide = rows[...].astype(F32)
    scaled = (wide * gain[...]).astype(BF)
    scaled_out[...] = scaled
    at = 0
    for weight in weights:
        width = weight.shape[1]
        out[:, at : at + width] = jnp.dot(
            scaled, weight[...], preferred_element_type=F32
        ).astype(BF)
        at += width
    out[:, at:] = lanes_of(jnp.sum(wide * wide, axis=1, keepdims=True))


def project(rows, gain, weights, widths, columns, limit_mib, name):
    count, depth = rows.shape
    out_width = sum(widths) + LANES
    tile = count // 2

    def weight_spec(i, width):
        return pl.BlockSpec((depth, width), lambda r, scalars: (0, scalars[i]))

    return pl.pallas_call(
        project_kernel,
        out_shape=[
            jax.ShapeDtypeStruct((count, out_width), BF),
            jax.ShapeDtypeStruct((count, depth), BF),
        ],
        grid_spec=pltpu.PrefetchScalarGridSpec(
            num_scalar_prefetch=1,
            grid=(2,),
            in_specs=[
                pl.BlockSpec((tile, depth), lambda r, scalars: (r, 0)),
                pl.BlockSpec((1, depth), lambda r, scalars: (0, 0)),
            ]
            + [weight_spec(i, width) for i, width in enumerate(widths)],
            out_specs=[
                pl.BlockSpec((tile, out_width), lambda r, scalars: (r, 0)),
                pl.BlockSpec((tile, depth), lambda r, scalars: (r, 0)),
            ],
        ),
        compiler_params=params(limit_mib),
        cost_estimate=cost(2 * count * depth * out_width, 2 * out_width * (count + depth)),
        name=name,
    )(jnp.stack(columns).astype(jnp.int32), rows, gain.reshape(1, depth), *weights)


def copies_kernel(body, scalars, *refs):
    *ins, out = refs
    value = body(*ins)
    for i in range(out.shape[0]):
        out[i] = value


def summed_copies(body, ins, in_specs, scalars, copies, rows, width, name):
    return pl.pallas_call(
        functools.partial(copies_kernel, body),
        out_shape=jax.ShapeDtypeStruct((copies, rows, width), BF),
        grid_spec=pltpu.PrefetchScalarGridSpec(
            num_scalar_prefetch=1,
            grid=(1,),
            in_specs=in_specs,
            out_specs=pl.BlockSpec((copies, rows, width), lambda i, scalars: (0, 0, 0)),
        ),
        compiler_params=params(12),
        cost_estimate=cost(0, 4 * copies * rows * width),
        name=name,
    )(scalars, *ins)


def whole(array):
    return pl.BlockSpec(array.shape, lambda i, scalars: (0,) * array.ndim)


def qkv_body(received):
    total = jnp.sum(received[...].astype(F32), axis=0)
    width = total.shape[1] - LANES
    squares = total[:, width : width + 1] + total[:, width + 1 : width + 2]
    return (total[:, :width] * lax.rsqrt(squares / D + EPSILON)).astype(BF)


def residual_body(received, rows):
    return (rows[...].astype(F32) + jnp.sum(received[...].astype(F32), axis=0)).astype(BF)


def sums_kernel(scalars, received, scaled_res, payload, minus_hidden):
    ff_dev = minus_hidden.shape[1]
    rows = received.shape[1]
    total = jnp.sum(received[...].astype(F32), axis=0)
    squares = total[:, 2 * ff_dev : 2 * ff_dev + 1] + total[:, 2 * ff_dev + 1 : 2 * ff_dev + 2]
    scale = lax.rsqrt(squares / D + EPSILON)
    gate = total[:, :ff_dev] * scale
    up = total[:, ff_dev : 2 * ff_dev] * scale
    minus_hidden[...] = (-(gate * jax.nn.sigmoid(gate) * up)).astype(BF)
    parts = (gate[:, :CAND_DEV].astype(BF), up[:, :CAND_DEV].astype(BF), lanes_of(scale), scaled_res)
    at = 0
    for part in parts:
        count = part.shape[0]
        for lane in range(0, part.shape[1], LANES):
            payload[at : at + count, :] = part[:, lane : lane + LANES]
            at += count


def gate_up_sums(scalars, received, scaled_res):
    _, rows, width = received.shape
    ff_dev = (width - LANES) // 2
    half, depth = scaled_res.shape[0] // 2, scaled_res.shape[1]
    payload_rows = rows * SUMS_TILES + half * (depth // LANES)
    return pl.pallas_call(
        sums_kernel,
        out_shape=[
            jax.ShapeDtypeStruct((payload_rows, LANES), BF),
            jax.ShapeDtypeStruct((rows, ff_dev), BF),
        ],
        grid_spec=pltpu.PrefetchScalarGridSpec(
            num_scalar_prefetch=1,
            grid=(1,),
            in_specs=[
                whole(received),
                pl.BlockSpec((half, depth), lambda i, scalars: (scalars[0], 0)),
            ],
            out_specs=[
                pl.BlockSpec((payload_rows, LANES), lambda i, scalars: (0, 0)),
                pl.BlockSpec((rows, ff_dev), lambda i, scalars: (0, 0)),
            ],
        ),
        compiler_params=params(20),
        cost_estimate=cost(0, 4 * received.size, rows * ff_dev),
        name="gate_up_sums",
    )(scalars, received, scaled_res)


LIVE_AT, LIVES_AT, Z_AT = 1, 2, 10
SUMS_TILES = 2 * CAND_DEV // LANES + 1


def dropped_kernel(scalars, own, other, down, down_rest, out, rows):
    cands, _, chunks, chunk, width = out.shape

    @pl.when(pl.program_id(0) == 0)
    def _():
        own_first = scalars[Z_AT] == 0
        unit = lax.broadcasted_iota(jnp.int32, (chunk, own.shape[1]), 1)
        for at in range(4):
            part = slice(at % 2 * chunk, (at % 2 + 1) * chunk)
            here, there = own[part, :].astype(F32), other[part, :].astype(F32)
            values = jnp.where(own_first == (at < 2), here, there)
            for c in range(8):
                kept = jnp.where(unit >= scalars[LIVES_AT + c], values, 0.0).astype(BF)
                rows[(c * 4 + at) * chunk : (c * 4 + at + 1) * chunk, :] = kept

    total = jnp.dot(rows[:, :CAND_DEV], down[0], preferred_element_type=F32)
    total += jnp.dot(rows[:, CAND_DEV:], down_rest[0], preferred_element_type=F32)
    out[:, 0] = total.astype(BF).reshape(cands, chunks, chunk, width)


def dropped_output(scalars, own, other, down_four, flip):
    tok_cand, ff_dev = own.shape
    width = down_four.shape[2]
    chunk = tok_cand // 2
    rest = ff_dev - CAND_DEV

    def block(i, scalars):
        return 2 * (1 - scalars[0] if flip else scalars[0]) + i

    return pl.pallas_call(
        dropped_kernel,
        out_shape=jax.ShapeDtypeStruct((8, 2, 4, chunk, width), BF),
        grid_spec=pltpu.PrefetchScalarGridSpec(
            num_scalar_prefetch=1,
            grid=(2,),
            in_specs=[
                whole(own),
                whole(other),
                pl.BlockSpec((1, CAND_DEV, width), lambda i, scalars: (block(i, scalars), 0, 0)),
                pl.BlockSpec(
                    (1, rest, width),
                    lambda i, scalars: (block(i, scalars), 2 * CAND_DEV // rest, 0),
                ),
            ],
            out_specs=pl.BlockSpec(
                (8, 1, 4, chunk, width), lambda i, scalars: (0, i, 0, 0, 0)
            ),
            scratch_shapes=[pltpu.VMEM((32 * chunk, ff_dev), BF)],
        ),
        compiler_params=params(60),
        cost_estimate=cost(4 * 32 * chunk * ff_dev * width, 4 * (ff_dev + 32 * chunk) * width),
        name="dropped_output",
    )(scalars, own, other, down_four, down_four)


def tiles_of(block, first, count, rows):
    tiles = [block[..., first + i * rows : first + (i + 1) * rows, :] for i in range(count)]
    return jnp.concatenate([tile.reshape(-1, LANES) for tile in tiles], axis=1)


def factors_kernel(rows, scalars, payload, gate_factor, up_factor, used_t):
    payload = payload[...]
    tiles = CAND_DEV // LANES
    gate = tiles_of(payload, 0, tiles, rows).astype(F32)
    up = tiles_of(payload, tiles * rows, tiles, rows).astype(F32)
    keep = lax.broadcasted_iota(jnp.int32, gate.shape, 1) < scalars[LIVE_AT]
    scale = jnp.where(keep, column_of(tiles_of(payload, 2 * tiles * rows, 1, rows)), 0.0)
    sigmoid = jax.nn.sigmoid(gate)
    activated = gate * sigmoid
    slope = sigmoid * (1.0 + gate * (1.0 - sigmoid))
    gate_factor[...] = up * slope * scale
    up_factor[...] = activated * scale
    used_t[...] = jnp.where(keep, activated * up, 0.0).T.astype(BF)


def factors(scalars, gathered, rows):
    cands, payload_rows, _ = gathered.shape
    tok_count = cands * rows
    half = tok_count // 2
    factor = jax.ShapeDtypeStruct((tok_count, CAND_DEV), F32)
    return pl.pallas_call(
        functools.partial(factors_kernel, rows),
        out_shape=[factor, factor, jax.ShapeDtypeStruct((CAND_DEV, tok_count), BF)],
        grid_spec=pltpu.PrefetchScalarGridSpec(
            num_scalar_prefetch=1,
            grid=(2,),
            in_specs=[
                pl.BlockSpec(
                    (cands // 2, payload_rows, LANES),
                    lambda i, scalars: ((scalars[0] + i) % 2, 0, 0),
                ),
            ],
            out_specs=[
                pl.BlockSpec((half, CAND_DEV), lambda i, scalars: (i, 0)),
                pl.BlockSpec((half, CAND_DEV), lambda i, scalars: (i, 0)),
                pl.BlockSpec((CAND_DEV, half), lambda i, scalars: (0, i)),
            ],
        ),
        compiler_params=params(28),
        cost_estimate=cost(0, 2 * gathered.size + 10 * tok_count * CAND_DEV, tok_count * CAND_DEV),
        name="factors",
    )(scalars, gathered)


def sum_error_kernel(received, out):
    value = jnp.sum(received[...].astype(F32), axis=1).astype(BF)
    for i in range(out.shape[0]):
        out[i] = value


def sum_error(received):
    groups, chips, rows, width = received.shape
    return pl.pallas_call(
        sum_error_kernel,
        out_shape=jax.ShapeDtypeStruct((chips, groups, rows, width), BF),
        grid=(4,),
        in_specs=[pl.BlockSpec((groups // 4, chips, rows, width), lambda i: (i, 0, 0, 0))],
        out_specs=pl.BlockSpec((chips, groups // 4, rows, width), lambda i: (0, i, 0, 0)),
        compiler_params=params(12),
        cost_estimate=cost(0, 4 * received.size),
        name="sum_error",
    )(received)


def contract(left, right, left_dim, right_dim):
    return lax.dot_general(
        left, right, (((left_dim,), (right_dim,)), ((), ())), preferred_element_type=F32
    )


def grad_rows_of(halves, z):
    rows = []
    for half in halves:
        block = half[0, :, z]
        rows += [block[chunk, y] for y in range(block.shape[1]) for chunk in range(block.shape[0])]
    return jnp.concatenate(rows, axis=0)


def back_product(scalars, halves, down):
    total = None
    for z in range(2):
        at = pl.multiple_of(jnp.where(scalars[Z_AT] == z, 0, CAND_DEV), CAND_DEV)
        product = contract(grad_rows_of(halves, z), down[0, pl.ds(at, CAND_DEV), :], 1, 1)
        total = product if total is None else total + product
    return total


def back_kernel(scalars, own_1, own_2, down, out):
    product = back_product(scalars, (own_1, own_2), down)

    @pl.when(pl.program_id(0) == 0)
    def _():
        out[...] = product

    @pl.when(pl.program_id(0) > 0)
    def _():
        out[...] += product


def half_specs(grad, block):
    chunks, z, y, rows, width = grad.shape[1:]

    def spec(flip):
        return pl.BlockSpec(
            (1, chunks // 2, z, y, rows, width),
            lambda i, scalars: (block(i), 1 - scalars[0] if flip else scalars[0], 0, 0, 0, 0),
        )

    return [spec(False), spec(True)]


def own_back(scalars, grad_own, down_four):
    _, chunks, z, y, rows, width = grad_own.shape
    tok_count = chunks * y * rows
    return pl.pallas_call(
        back_kernel,
        out_shape=jax.ShapeDtypeStruct((tok_count, CAND_DEV), F32),
        grid_spec=pltpu.PrefetchScalarGridSpec(
            num_scalar_prefetch=1,
            grid=(2,),
            in_specs=half_specs(grad_own, lambda i: i)
            + [
                pl.BlockSpec(
                    (1, 2 * CAND_DEV, width), lambda i, scalars: (2 * scalars[0] + i, 0, 0)
                )
            ],
            out_specs=pl.BlockSpec((tok_count, CAND_DEV), lambda i, scalars: (0, 0)),
        ),
        compiler_params=params(60),
        cost_estimate=cost(8 * tok_count * width * CAND_DEV, 10 << 20),
        name="own_back",
    )(scalars, grad_own, grad_own, down_four)


def gradient_kernel(
    scalars, own_1, own_2, other_1, other_2, down, res_1, res_2, start, gate_factor, up_factor, used_t, *refs
):
    gate_out, up_out, down_out, back, terms = refs
    step = pl.program_id(0)
    half, width = back.shape[0] // 2, own_1.shape[5]

    @pl.when(step == 0)
    def _():
        back[...] = start[...] + back_product(scalars, (other_1, other_2), down)

    @pl.when(step == 1)
    def _():
        total = back[...] + back_product(scalars, (other_1, other_2), down)
        terms[:, :CAND_DEV] = (total * gate_factor[...]).astype(BF)
        terms[:, CAND_DEV:] = (total * up_factor[...]).astype(BF)

    for at, halves in enumerate(((own_1, own_2), (other_1, other_2))):
        for z in range(2):

            @pl.when((step >= 2) & ((step - 2) // 4 == at) & ((step - 2) % 2 == z))
            def _(halves=halves, z=z):
                grad = grad_rows_of(halves, z)
                down_out[0] = jnp.dot(used_t[...], grad, preferred_element_type=F32).astype(BF)

    @pl.when(step >= 2)
    def _():
        tiles = width // LANES
        first = res_1.shape[1] - half * tiles
        res = [tiles_of(ref[0], first, tiles, half) for ref in (res_1, res_2)]
        res = jnp.concatenate(res, axis=0)
        both = contract(res, terms[...], 0, 0).astype(BF)
        gate_out[0] = both[:, :CAND_DEV]
        up_out[0] = both[:, CAND_DEV:]


def gradients(scalars, grad_own, grad_other, down_four, res_1, res_2, start, gate_factor, up_factor, used_t):
    _, chunks, z, y, rows, width = grad_own.shape
    tok_count = chunks * y * rows
    groups = 8

    def own_block(i):
        return jnp.clip((i - 2) // 2, 0, 1)

    def other_block(i):
        return jnp.where(i < 2, i, jnp.clip((i - 6) // 2, 0, 1))

    def late(i, scalars):
        at = jnp.maximum(i - 2, 0)
        core = jnp.where(at < 4, scalars[0], 1 - scalars[0])
        return at % 2 * 4 + 2 * core + at // 2 % 2

    res_spec = pl.BlockSpec((1,) + res_1.shape[1:], lambda i, scalars: (late(i, scalars), 0, 0))
    product = 2 * tok_count * groups * width * CAND_DEV
    return pl.pallas_call(
        gradient_kernel,
        out_shape=[
            jax.ShapeDtypeStruct((1, groups * width, CAND_DEV), BF),
            jax.ShapeDtypeStruct((1, groups * width, CAND_DEV), BF),
            jax.ShapeDtypeStruct((1, CAND_DEV, groups * width), BF),
        ],
        grid_spec=pltpu.PrefetchScalarGridSpec(
            num_scalar_prefetch=1,
            grid=(10,),
            in_specs=half_specs(grad_own, own_block)
            + half_specs(grad_other, other_block)
            + [
                pl.BlockSpec(
                    (1, 2 * CAND_DEV, width),
                    lambda i, scalars: (2 * (1 - scalars[0]) + jnp.minimum(i, 1), 0, 0),
                ),
                res_spec,
                res_spec,
                whole(start),
                whole(gate_factor),
                whole(up_factor),
                whole(used_t),
            ],
            out_specs=[
                pl.BlockSpec((1, width, CAND_DEV), lambda i, scalars: (0, late(i, scalars), 0)),
                pl.BlockSpec((1, width, CAND_DEV), lambda i, scalars: (0, late(i, scalars), 0)),
                pl.BlockSpec((1, CAND_DEV, width), lambda i, scalars: (0, 0, late(i, scalars))),
            ],
            scratch_shapes=[
                pltpu.VMEM((tok_count, CAND_DEV), F32),
                pltpu.VMEM((tok_count, 2 * CAND_DEV), BF),
            ],
        ),
        compiler_params=params(48),
        cost_estimate=cost(7 * product // 2, 40 << 20),
        name="gradients",
    )(
        scalars,
        grad_own,
        grad_own,
        grad_other,
        grad_other,
        down_four,
        res_1,
        res_2,
        start,
        gate_factor,
        up_factor,
        used_t,
    )


def shards(
    tokens,
    attn_gain,
    ffn_gain,
    w_query,
    w_key,
    w_value,
    w_out,
    w_gate,
    w_up,
    w_down,
    doc_ids,
    widths,
):
    cand_index = lax.axis_index("cand")
    tp_index = lax.axis_index("tp")
    core = (tp_index % 2).astype(jnp.int32)
    cands = lax.axis_size("cand")
    tps = lax.axis_size("tp")
    tok_count, width = tokens.shape
    ff_dev = w_gate.shape[1]
    tok_cand = tok_count // cands
    tok_tp = tok_count // tps
    nothing = jnp.zeros((1,), jnp.int32)

    down_across = lax.ppermute(w_down[:CAND_DEV], "cand", ACROSS_Z)

    heads_dev = w_query.shape[1] // HEAD_DIM
    kv_index = tp_index * heads_dev // (HEADS // KV_HEADS)
    zero = jnp.zeros_like(kv_index)
    q_width = heads_dev * HEAD_DIM
    part, _ = project(
        tokens,
        attn_gain,
        (w_query, w_key, w_value),
        (q_width, HEAD_DIM, HEAD_DIM),
        (zero, kv_index, kv_index),
        60,
        "project_qkv",
    )
    received = exchange(part.reshape(cands, tok_cand, part.shape[1]), "cand")
    received, down_across = lax.optimization_barrier((received, down_across))
    down_block = jnp.concatenate([w_down[:CAND_DEV], down_across, w_down[CAND_DEV:]], axis=0)
    down_four = lax.all_gather(down_block, "cand", axis=0, axis_index_groups=SAME_Z)
    qkv_width = part.shape[1] - LANES
    copies = summed_copies(
        qkv_body, (received,), [whole(received)], nothing, cands, tok_cand, qkv_width, "sum_qkv"
    )
    qkv = exchange(copies, "cand").reshape(tok_count, qkv_width)
    query = qkv[:, :q_width].reshape(tok_count, heads_dev, HEAD_DIM)
    key_rows = qkv[:, q_width : q_width + HEAD_DIM]
    value_rows = qkv[:, q_width + HEAD_DIM :]

    scores = jnp.einsum(
        "qhd,kd->hqk", query, key_rows, preferred_element_type=F32
    ) * HEAD_DIM ** (-0.5)
    position = lax.iota(jnp.int32, tok_count)
    allowed = (position[None, :] <= position[:, None]) & (doc_ids[None, :] == doc_ids[:, None])
    scores = jnp.where(allowed[None], scores, -1e30)
    peak_score = jnp.max(scores, axis=-1, keepdims=True)
    expo = jnp.exp(scores - peak_score)
    weights_bf = (expo / jnp.sum(expo, axis=-1, keepdims=True)).astype(BF)
    attended = jnp.einsum("hqk,kd->qhd", weights_bf, value_rows, preferred_element_type=F32)
    attended = attended.astype(BF).reshape(tok_count, heads_dev * HEAD_DIM)
    out_part = jnp.dot(attended, w_out, preferred_element_type=F32).astype(BF)
    received = exchange(out_part.reshape(tps, tok_tp, width), "tp")
    copies = summed_copies(
        residual_body,
        (received, tokens),
        [
            whole(received),
            pl.BlockSpec((tok_tp, width), lambda i, scalars: (scalars[0], 0)),
        ],
        tp_index.astype(jnp.int32)[None],
        tps,
        tok_tp,
        width,
        "sum_attention",
    )
    residual = exchange(copies, "tp").reshape(tok_count, width)

    part, scaled_res = project(
        residual, ffn_gain, (w_gate, w_up), (ff_dev, ff_dev), (zero, zero), 16, "project_gate_up"
    )
    received = exchange(part.reshape(cands, tok_cand, part.shape[1]), "cand")
    payload, minus_hidden = gate_up_sums(core[None], received, scaled_res)
    gathered = lax.all_gather(payload, "cand", axis=0)
    gathered_other = lax.ppermute(gathered, "tp", CORE_PAIRS)
    minus_hidden_across = lax.ppermute(minus_hidden, "cand", ACROSS_Z)

    live = (widths // tps).astype(jnp.int32)
    own_live = jnp.sum(jnp.where(lax.iota(jnp.int32, widths.shape[0]) == cand_index, live, 0))
    z_index = (cand_index // 4).astype(jnp.int32)
    scalars = jnp.concatenate([core[None], own_live[None], live, z_index[None]])
    for_other = dropped_output(scalars, minus_hidden, minus_hidden_across, down_four, True)
    away = lax.ppermute(for_other, "tp", CORE_PAIRS)
    mine = dropped_output(scalars, minus_hidden, minus_hidden_across, down_four, False)
    pair_sum = (mine.astype(F32) + away.astype(F32)).astype(BF)
    chunk = tok_cand // 2
    parts = pair_sum.reshape(cands * tps // 2, chunk, width)
    received = exchange(parts, ("cand", "tp"), SAME_CORE_ALL)
    copies = sum_error(received.reshape(cands, tps // 2, chunk, width))
    grad_own = exchange(copies, "tp", SAME_CORE).reshape(2, 4, 2, 4, chunk, width)
    grad_other = lax.ppermute(grad_own, "tp", CORE_PAIRS)

    start = own_back(scalars, grad_own, down_four)
    return tuple(
        gradients(
            scalars,
            grad_own,
            grad_other,
            down_four,
            gathered,
            gathered_other,
            start,
            *factors(scalars, gathered, tok_cand),
        )
    )


def solution(mesh):
    in_specs = (
        P(None, "cand"),
        P("cand"),
        P("cand"),
        P("cand", "tp"),
        P("cand", None),
        P("cand", None),
        P("tp", "cand"),
        P("cand", "tp"),
        P("cand", "tp"),
        P("tp", "cand"),
        P(),
        P(),
    )
    out_specs = (P("cand", None, "tp"), P("cand", None, "tp"), P("cand", "tp", None))
    return jax.shard_map(shards, mesh=mesh, in_specs=in_specs, out_specs=out_specs, check_vma=False)
```

```python
import functools

import jax
import jax.numpy as jnp
from jax import lax
from jax.experimental import pallas as pl
from jax.experimental.pallas import tpu as pltpu
from jax.sharding import PartitionSpec as P

D = 4096
HEADS = 32
KV_HEADS = 8
HEAD_DIM = 128
CAND_DEV = 768
LANES = 128
EPSILON = 1e-05
BF = jnp.bfloat16
F32 = jnp.float32

VMEM = pl.BlockSpec(memory_space=pltpu.VMEM)
CORE_PAIRS = [(i, i ^ 1) for i in range(16)]
ACROSS_Z = [(i, i ^ 4) for i in range(8)]
SAME_Z = [[0, 1, 2, 3], [4, 5, 6, 7]]
SAME_CORE_ALL = [[c * 16 + t for c in range(8) for t in range(core, 16, 2)] for core in range(2)]
SAME_CORE = [list(range(core, 16, 2)) for core in range(2)]


def exchange(blocks, axis, groups=None):
    return lax.all_to_all(blocks, axis, 0, 0, axis_index_groups=groups)


def lanes_of(column):
    high = column.astype(BF).astype(F32)
    lane = lax.broadcasted_iota(jnp.int32, (column.shape[0], LANES), 1)
    return jnp.where(lane == 0, high, jnp.where(lane == 1, column - high, 0.0)).astype(BF)


def column_of(lanes):
    return lanes[:, 0:1].astype(F32) + lanes[:, 1:2].astype(F32)


def params(limit_mib):
    return pltpu.CompilerParams(
        dimension_semantics=("arbitrary",), vmem_limit_bytes=limit_mib << 20
    )


def cost(flops, bytes_accessed, transcendentals=0):
    return pl.CostEstimate(
        flops=flops, bytes_accessed=bytes_accessed, transcendentals=transcendentals
    )


def project_kernel(scalars, rows, gain, *refs):
    *weights, out, scaled_out = refs
    wide = rows[...].astype(F32)
    scaled = (wide * gain[...]).astype(BF)
    scaled_out[...] = scaled
    at = 0
    for weight in weights:
        width = weight.shape[1]
        out[:, at : at + width] = jnp.dot(
            scaled, weight[...], preferred_element_type=F32
        ).astype(BF)
        at += width
    out[:, at:] = lanes_of(jnp.sum(wide * wide, axis=1, keepdims=True))


def project(rows, gain, weights, widths, columns, limit_mib, name):
    count, depth = rows.shape
    out_width = sum(widths) + LANES
    tile = count // 2

    def weight_spec(i, width):
        return pl.BlockSpec((depth, width), lambda r, scalars: (0, scalars[i]))

    return pl.pallas_call(
        project_kernel,
        out_shape=[
            jax.ShapeDtypeStruct((count, out_width), BF),
            jax.ShapeDtypeStruct((count, depth), BF),
        ],
        grid_spec=pltpu.PrefetchScalarGridSpec(
            num_scalar_prefetch=1,
            grid=(2,),
            in_specs=[
                pl.BlockSpec((tile, depth), lambda r, scalars: (r, 0)),
                pl.BlockSpec((1, depth), lambda r, scalars: (0, 0)),
            ]
            + [weight_spec(i, width) for i, width in enumerate(widths)],
            out_specs=[
                pl.BlockSpec((tile, out_width), lambda r, scalars: (r, 0)),
                pl.BlockSpec((tile, depth), lambda r, scalars: (r, 0)),
            ],
        ),
        compiler_params=params(limit_mib),
        cost_estimate=cost(2 * count * depth * out_width, 2 * out_width * (count + depth)),
        name=name,
    )(jnp.stack(columns).astype(jnp.int32), rows, gain.reshape(1, depth), *weights)


def copies_kernel(body, scalars, *refs):
    *ins, out = refs
    value = body(*ins)
    for i in range(out.shape[0]):
        out[i] = value


def summed_copies(body, ins, in_specs, scalars, copies, rows, width, name):
    return pl.pallas_call(
        functools.partial(copies_kernel, body),
        out_shape=jax.ShapeDtypeStruct((copies, rows, width), BF),
        grid_spec=pltpu.PrefetchScalarGridSpec(
            num_scalar_prefetch=1,
            grid=(1,),
            in_specs=in_specs,
            out_specs=pl.BlockSpec((copies, rows, width), lambda i, scalars: (0, 0, 0)),
        ),
        compiler_params=params(12),
        cost_estimate=cost(0, 4 * copies * rows * width),
        name=name,
    )(scalars, *ins)


def whole(array):
    return pl.BlockSpec(array.shape, lambda i, scalars: (0,) * array.ndim)


def to_vmem_kernel(blocks, out):
    out[pl.program_id(0)] = blocks[0]


def to_vmem(blocks):
    return pl.pallas_call(
        to_vmem_kernel,
        out_shape=jax.ShapeDtypeStruct(blocks.shape, blocks.dtype),
        grid=(blocks.shape[0],),
        in_specs=[pl.BlockSpec((1,) + blocks.shape[1:], lambda i: (i, 0, 0))],
        out_specs=VMEM,
        compiler_params=params(12),
        cost_estimate=cost(0, 4 * blocks.size),
        name="to_vmem",
    )(blocks)


def qkv_body(received):
    total = jnp.sum(received[...].astype(F32), axis=0)
    width = total.shape[1] - LANES
    squares = total[:, width : width + 1] + total[:, width + 1 : width + 2]
    return (total[:, :width] * lax.rsqrt(squares / D + EPSILON)).astype(BF)


def residual_body(received, rows):
    return (rows[...].astype(F32) + jnp.sum(received[...].astype(F32), axis=0)).astype(BF)


def sums_kernel(scalars, received, scaled_res, res_across, payload, minus_hidden):
    ff_dev = minus_hidden.shape[1]
    rows = received.shape[1]
    total = jnp.sum(received[...].astype(F32), axis=0)
    squares = total[:, 2 * ff_dev : 2 * ff_dev + 1] + total[:, 2 * ff_dev + 1 : 2 * ff_dev + 2]
    scale = lax.rsqrt(squares / D + EPSILON)
    gate = total[:, :ff_dev] * scale
    up = total[:, ff_dev : 2 * ff_dev] * scale
    minus_hidden[...] = (-(gate * jax.nn.sigmoid(gate) * up)).astype(BF)
    parts = (gate[:, :CAND_DEV].astype(BF), up[:, :CAND_DEV].astype(BF), lanes_of(scale), scaled_res, res_across)
    at = 0
    for part in parts:
        count = part.shape[0]
        for lane in range(0, part.shape[1], LANES):
            payload[at : at + count, :] = part[:, lane : lane + LANES]
            at += count


def gate_up_sums(scalars, received, scaled_res, res_across):
    _, rows, width = received.shape
    ff_dev = (width - LANES) // 2
    half, depth = scaled_res.shape[0] // 2, scaled_res.shape[1]
    payload_rows = rows * SUMS_TILES + 2 * half * (depth // LANES)
    return pl.pallas_call(
        sums_kernel,
        out_shape=[
            jax.ShapeDtypeStruct((payload_rows, LANES), BF),
            jax.ShapeDtypeStruct((rows, ff_dev), BF),
        ],
        grid_spec=pltpu.PrefetchScalarGridSpec(
            num_scalar_prefetch=1,
            grid=(1,),
            in_specs=[
                whole(received),
                pl.BlockSpec((half, depth), lambda i, scalars: (scalars[0], 0)),
                whole(res_across),
            ],
            out_specs=[
                pl.BlockSpec((payload_rows, LANES), lambda i, scalars: (0, 0)),
                pl.BlockSpec((rows, ff_dev), lambda i, scalars: (0, 0)),
            ],
        ),
        compiler_params=params(20),
        cost_estimate=cost(0, 4 * received.size, rows * ff_dev),
        name="gate_up_sums",
    )(scalars, received, scaled_res, res_across)


LIVE_AT, LIVES_AT, Z_AT = 1, 2, 10
SUMS_TILES = 2 * CAND_DEV // LANES + 1


def dropped_kernel(flip, scalars, own, other, down, out, rows):
    cands, _, chunks, chunk, width = out.shape

    @pl.when(pl.program_id(0) == 0)
    def _():
        own_first = scalars[Z_AT] == 0
        unit = lax.broadcasted_iota(jnp.int32, (chunk, own.shape[1]), 1)
        for at in range(4):
            part = slice(at % 2 * chunk, (at % 2 + 1) * chunk)
            here, there = own[part, :].astype(F32), other[part, :].astype(F32)
            values = jnp.where(own_first == (at < 2), here, there)
            for c in range(8):
                kept = jnp.where(unit >= scalars[LIVES_AT + c], values, 0.0).astype(BF)
                rows[(c * 4 + at) * chunk : (c * 4 + at + 1) * chunk, :] = kept

    block = 2 * (1 - scalars[0] if flip else scalars[0]) + pl.program_id(0)
    total = jnp.dot(rows[...], down[block], preferred_element_type=F32)
    out[:, 0] = total.astype(BF).reshape(cands, chunks, chunk, width)


def dropped_output(scalars, own, other, down_four, flip):
    tok_cand, ff_dev = own.shape
    width = down_four.shape[2]
    chunk = tok_cand // 2

    return pl.pallas_call(
        functools.partial(dropped_kernel, flip),
        out_shape=jax.ShapeDtypeStruct((8, 2, 4, chunk, width), BF),
        grid_spec=pltpu.PrefetchScalarGridSpec(
            num_scalar_prefetch=1,
            grid=(2,),
            in_specs=[
                whole(own),
                whole(other),
                VMEM,
            ],
            out_specs=pl.BlockSpec(
                (8, 1, 4, chunk, width), lambda i, scalars: (0, i, 0, 0, 0)
            ),
            scratch_shapes=[pltpu.VMEM((32 * chunk, ff_dev), BF)],
        ),
        compiler_params=params(20),
        cost_estimate=cost(4 * 32 * chunk * ff_dev * width, 4 * (ff_dev + 32 * chunk) * width),
        name="dropped_output",
    )(scalars, own, other, down_four)


def tiles_of(block, first, count, rows):
    tiles = [block[..., first + i * rows : first + (i + 1) * rows, :] for i in range(count)]
    return jnp.concatenate([tile.reshape(-1, LANES) for tile in tiles], axis=1)


def factors_kernel(rows, scalars, own_sums, across_sums, gate_factor, up_factor, used_t):
    own_z = (scalars[0] + pl.program_id(0)) % 2 == scalars[Z_AT]
    payload = jnp.where(own_z, own_sums[...].astype(F32), across_sums[...].astype(F32))
    tiles = CAND_DEV // LANES
    gate = tiles_of(payload, 0, tiles, rows)
    up = tiles_of(payload, tiles * rows, tiles, rows)
    keep = lax.broadcasted_iota(jnp.int32, gate.shape, 1) < scalars[LIVE_AT]
    scale = jnp.where(keep, column_of(tiles_of(payload, 2 * tiles * rows, 1, rows)), 0.0)
    sigmoid = jax.nn.sigmoid(gate)
    activated = gate * sigmoid
    slope = sigmoid * (1.0 + gate * (1.0 - sigmoid))
    at = pl.program_id(0)
    half = gate.shape[0]
    gate_factor[pl.ds(at * half, half), :] = (up * slope * scale).astype(BF)
    up_factor[pl.ds(at * half, half), :] = (activated * scale).astype(BF)
    turned = jnp.where(keep, activated * up, 0.0).T.astype(BF)
    used_t[:, pl.ds(pl.multiple_of(at * half, half), half)] = turned


def factors(scalars, own_sums, across_sums, rows):
    groups = own_sums.shape[0]
    half = groups * rows
    tok_count = 2 * half
    factor = jax.ShapeDtypeStruct((tok_count, CAND_DEV), BF)
    return pl.pallas_call(
        functools.partial(factors_kernel, rows),
        out_shape=[factor, factor, jax.ShapeDtypeStruct((CAND_DEV, tok_count), BF)],
        grid_spec=pltpu.PrefetchScalarGridSpec(
            num_scalar_prefetch=1,
            grid=(2,),
            in_specs=[
                pl.BlockSpec((groups, rows * SUMS_TILES, LANES), lambda i, scalars: (0, 0, 0)),
            ]
            + [
                pl.BlockSpec((groups, rows * SUMS_TILES, LANES), lambda i, scalars: (0, 0, 0)),
            ],
            out_specs=[VMEM] * 3,
        ),
        compiler_params=params(24),
        cost_estimate=cost(0, 14 * tok_count * CAND_DEV, tok_count * CAND_DEV),
        name="factors",
    )(scalars, own_sums, across_sums)


def sum_error_kernel(received, out):
    value = jnp.sum(received[...].astype(F32), axis=1).astype(BF)
    for i in range(out.shape[0]):
        out[i] = value


def sum_error(received):
    groups, chips, rows, width = received.shape
    return pl.pallas_call(
        sum_error_kernel,
        out_shape=jax.ShapeDtypeStruct((chips, groups, rows, width), BF),
        grid=(4,),
        in_specs=[pl.BlockSpec((groups // 4, chips, rows, width), lambda i: (i, 0, 0, 0))],
        out_specs=pl.BlockSpec((chips, groups // 4, rows, width), lambda i: (0, i, 0, 0)),
        compiler_params=params(12),
        cost_estimate=cost(0, 4 * received.size),
        name="sum_error",
    )(received)


def contract(left, right, left_dim, right_dim):
    return lax.dot_general(
        left, right, (((left_dim,), (right_dim,)), ((), ())), preferred_element_type=F32
    )


def grad_rows_of(scalars, grad, block, z):
    rows = []
    for half in (scalars[0], 1 - scalars[0]):
        for y in range(grad.shape[3]):
            rows += [grad[block, 2 * half + i, z, y] for i in range(2)]
    return jnp.concatenate(rows, axis=0)


def back_product(scalars, grad, own_four, across_four, core):
    total = None
    for z, down in ((scalars[Z_AT], own_four), (1 - scalars[Z_AT], across_four)):
        rows = [grad_rows_of(scalars, grad, block, z) for block in range(2)]
        units = [down[2 * core + block, :CAND_DEV] for block in range(2)]
        product = contract(jnp.concatenate(rows, axis=1), jnp.concatenate(units, axis=1), 1, 1)
        total = product if total is None else total + product
    return total


def back_kernel(scalars, grad, own_four, across_four, out):
    out[...] = back_product(scalars, grad, own_four, across_four, scalars[0])


def own_back(scalars, grad_own, own_four, across_four):
    _, chunks, z, y, rows, width = grad_own.shape
    tok_count = chunks * y * rows
    return pl.pallas_call(
        back_kernel,
        out_shape=jax.ShapeDtypeStruct((tok_count, CAND_DEV), F32),
        in_specs=[pl.BlockSpec(memory_space=pltpu.SMEM), VMEM, VMEM, VMEM],
        out_specs=VMEM,
        compiler_params=pltpu.CompilerParams(vmem_limit_bytes=16 << 20),
        cost_estimate=cost(8 * tok_count * width * CAND_DEV, 10 << 20),
        name="own_back",
    )(scalars, grad_own, own_four, across_four)


def res_order_kernel(half, first_row, scalars, first, second, out):
    at = pl.program_id(0)
    tiles = out.shape[2] // LANES
    for part in range(2):
        z = jnp.where(scalars[Z_AT] == 0, part, 1 - part)
        start = first_row + part * half * tiles
        for row, ref in ((0, first), (half, second)):
            out[4 * z + at, row : row + half, :] = tiles_of(ref[0], start, tiles, half)


def res_order(scalars, gathered, gathered_other, first_row, half, width):
    blocks = gathered.shape[0]
    spec = pl.BlockSpec((1,) + gathered.shape[1:], lambda i, scalars: (i, 0, 0))
    return pl.pallas_call(
        functools.partial(res_order_kernel, half, first_row),
        out_shape=jax.ShapeDtypeStruct((2 * blocks, 2 * half, width), BF),
        grid_spec=pltpu.PrefetchScalarGridSpec(
            num_scalar_prefetch=1, grid=(blocks,), in_specs=[spec, spec], out_specs=VMEM
        ),
        compiler_params=params(16),
        cost_estimate=cost(0, 4 * gathered.size + 8 * blocks * half * width),
        name="res_order",
    )(scalars, gathered, gathered_other)


def gradient_kernel(
    scalars, own, other, own_four, across_four, res, start, gate_factor, up_factor, used_t, gate_out, up_out, down_out, terms
):
    step = pl.program_id(0)

    @pl.when(step == 0)
    def _():
        total = start[...] + back_product(scalars, other, own_four, across_four, 1 - scalars[0])
        terms[:, :CAND_DEV] = (total * gate_factor[...].astype(F32)).astype(BF)
        terms[:, CAND_DEV:] = (total * up_factor[...].astype(F32)).astype(BF)

    for at, grad in enumerate((own, other)):

        @pl.when((step >= 1) & (step < 5) & ((step - 1) // 2 == at))
        def _(grad=grad):
            z = (step - 1) % 2
            rows = [grad_rows_of(scalars, grad, block, z) for block in range(2)]
            rows = jnp.concatenate(rows, axis=1)
            down_out[0] = jnp.dot(used_t[...], rows, preferred_element_type=F32).astype(BF)

    @pl.when(step >= 5)
    def _():
        both = contract(res[jnp.maximum(step - 5, 0)], terms[...], 0, 0).astype(BF)
        gate_out[0] = both[:, :CAND_DEV]
        up_out[0] = both[:, CAND_DEV:]


def gradients(
    scalars, grad_own, grad_other, own_four, across_four, res, start, gate_factor, up_factor, used_t
):
    groups, tok_count, width = res.shape

    def late_pair(i, scalars):
        at = jnp.clip(i - 1, 0, 3)
        return at % 2 * 2 + jnp.where(at < 2, scalars[0], 1 - scalars[0])

    out = jax.ShapeDtypeStruct((1, groups * width, CAND_DEV), BF)
    out_spec = pl.BlockSpec((1, width, CAND_DEV), lambda i, scalars: (0, jnp.maximum(i - 5, 0), 0))
    product = 2 * tok_count * groups * width * CAND_DEV
    return pl.pallas_call(
        gradient_kernel,
        out_shape=[out, out, jax.ShapeDtypeStruct((1, CAND_DEV, groups * width), BF)],
        grid_spec=pltpu.PrefetchScalarGridSpec(
            num_scalar_prefetch=1,
            grid=(5 + groups,),
            in_specs=[VMEM] * 9,
            out_specs=[
                out_spec,
                out_spec,
                pl.BlockSpec(
                    (1, CAND_DEV, 2 * width), lambda i, scalars: (0, 0, late_pair(i, scalars))
                ),
            ],
            scratch_shapes=[pltpu.VMEM((tok_count, 2 * CAND_DEV), BF)],
        ),
        compiler_params=params(28),
        cost_estimate=cost(7 * product // 2, 40 << 20),
        name="gradients",
    )(
        scalars,
        grad_own,
        grad_other,
        own_four,
        across_four,
        res,
        start,
        gate_factor,
        up_factor,
        used_t,
    )


def shards(
    tokens,
    attn_gain,
    ffn_gain,
    w_query,
    w_key,
    w_value,
    w_out,
    w_gate,
    w_up,
    w_down,
    doc_ids,
    widths,
):
    cand_index = lax.axis_index("cand")
    tp_index = lax.axis_index("tp")
    core = (tp_index % 2).astype(jnp.int32)
    cands = lax.axis_size("cand")
    tps = lax.axis_size("tp")
    tok_count, width = tokens.shape
    ff_dev = w_gate.shape[1]
    tok_cand = tok_count // cands
    tok_tp = tok_count // tps
    nothing = jnp.zeros((1,), jnp.int32)

    own_four = lax.all_gather(w_down, "cand", axis=0, axis_index_groups=SAME_Z)
    down_across = lax.ppermute(w_down[:CAND_DEV], "cand", ACROSS_Z)

    heads_dev = w_query.shape[1] // HEAD_DIM
    kv_index = tp_index * heads_dev // (HEADS // KV_HEADS)
    zero = jnp.zeros_like(kv_index)
    q_width = heads_dev * HEAD_DIM
    part, _ = project(
        tokens,
        attn_gain,
        (w_query, w_key, w_value),
        (q_width, HEAD_DIM, HEAD_DIM),
        (zero, kv_index, kv_index),
        60,
        "project_qkv",
    )
    received = exchange(part.reshape(cands, tok_cand, part.shape[1]), "cand")
    received, down_across = lax.optimization_barrier((received, down_across))
    across_four = lax.all_gather(down_across, "cand", axis=0, axis_index_groups=SAME_Z)
    qkv_width = part.shape[1] - LANES
    copies = summed_copies(
        qkv_body, (received,), [whole(received)], nothing, cands, tok_cand, qkv_width, "sum_qkv"
    )
    qkv = exchange(copies, "cand").reshape(tok_count, qkv_width)
    query = qkv[:, :q_width].reshape(tok_count, heads_dev, HEAD_DIM)
    key_rows = qkv[:, q_width : q_width + HEAD_DIM]
    value_rows = qkv[:, q_width + HEAD_DIM :]

    scores = jnp.einsum(
        "qhd,kd->hqk", query, key_rows, preferred_element_type=F32
    ) * HEAD_DIM ** (-0.5)
    position = lax.iota(jnp.int32, tok_count)
    allowed = (position[None, :] <= position[:, None]) & (doc_ids[None, :] == doc_ids[:, None])
    scores = jnp.where(allowed[None], scores, -1e30)
    peak_score = jnp.max(scores, axis=-1, keepdims=True)
    expo = jnp.exp(scores - peak_score)
    weights_bf = (expo / jnp.sum(expo, axis=-1, keepdims=True)).astype(BF)
    attended = jnp.einsum("hqk,kd->qhd", weights_bf, value_rows, preferred_element_type=F32)
    attended = attended.astype(BF).reshape(tok_count, heads_dev * HEAD_DIM)
    out_part = jnp.dot(attended, w_out, preferred_element_type=F32).astype(BF)
    received = exchange(out_part.reshape(tps, tok_tp, width), "tp")
    copies = summed_copies(
        residual_body,
        (received, tokens),
        [
            whole(received),
            pl.BlockSpec((tok_tp, width), lambda i, scalars: (scalars[0], 0)),
        ],
        tp_index.astype(jnp.int32)[None],
        tps,
        tok_tp,
        width,
        "sum_attention",
    )
    residual = exchange(copies, "tp").reshape(tok_count, width)

    residual, own_four = lax.optimization_barrier((residual, own_four))
    own_four = to_vmem(own_four)
    part, scaled_res = project(
        residual, ffn_gain, (w_gate, w_up), (ff_dev, ff_dev), (zero, zero), 16, "project_gate_up"
    )
    tok_half = tok_count // 2
    res_half = lax.dynamic_slice_in_dim(scaled_res, core * tok_half, tok_half, 0)
    res_across = lax.ppermute(res_half, "cand", ACROSS_Z)
    received = exchange(part.reshape(cands, tok_cand, part.shape[1]), "cand")
    received, own_four, res_across = lax.optimization_barrier((received, own_four, res_across))
    payload, minus_hidden = gate_up_sums(core[None], received, scaled_res, res_across)
    sums_rows = tok_cand * SUMS_TILES
    sums_across = lax.ppermute(payload[:sums_rows], "cand", ACROSS_Z)
    minus_hidden_across = lax.ppermute(minus_hidden, "cand", ACROSS_Z)

    live = (widths // tps).astype(jnp.int32)
    own_live = jnp.sum(jnp.where(lax.iota(jnp.int32, widths.shape[0]) == cand_index, live, 0))
    z_index = (cand_index // 4).astype(jnp.int32)
    scalars = jnp.concatenate([core[None], own_live[None], live, z_index[None]])
    minus_hidden, across_four = lax.optimization_barrier((minus_hidden, across_four))
    for_other = dropped_output(scalars, minus_hidden, minus_hidden_across, own_four, True)
    away = lax.ppermute(for_other, "tp", CORE_PAIRS)
    mine = dropped_output(scalars, minus_hidden, minus_hidden_across, own_four, False)
    pair_sum = (mine.astype(F32) + away.astype(F32)).astype(BF)
    pair_sum, sums_across = lax.optimization_barrier((pair_sum, sums_across))
    payload = jnp.concatenate([payload, sums_across], axis=0)
    gathered = lax.all_gather(payload, "cand", axis=0, axis_index_groups=SAME_Z)
    chunk = tok_cand // 2
    parts = pair_sum.reshape(cands * tps // 2, chunk, width)
    received = exchange(parts, ("cand", "tp"), SAME_CORE_ALL)
    copies = sum_error(received.reshape(cands, tps // 2, chunk, width))
    gathered_other = lax.ppermute(gathered, "tp", CORE_PAIRS)
    grad_own = exchange(copies, "tp", SAME_CORE).reshape(2, 4, 2, 4, chunk, width)
    grad_other = lax.ppermute(grad_own, "tp", CORE_PAIRS)

    res = res_order(scalars, gathered, gathered_other, sums_rows, tok_half, width)
    factor = factors(scalars, gathered[:, :sums_rows], gathered[:, -sums_rows:], tok_cand)
    across_four = to_vmem(across_four)
    grad_own, across_four, *factor = lax.optimization_barrier((grad_own, across_four, *factor))
    start = own_back(scalars, grad_own, own_four, across_four)
    return tuple(
        gradients(
            scalars, grad_own, grad_other, own_four, across_four, res, start, *factor
        )
    )


def solution(mesh):
    in_specs = (
        P(None, "cand"),
        P("cand"),
        P("cand"),
        P("cand", "tp"),
        P("cand", None),
        P("cand", None),
        P("tp", "cand"),
        P("cand", "tp"),
        P("cand", "tp"),
        P("tp", "cand"),
        P(),
        P(),
    )
    out_specs = (P("cand", None, "tp"), P("cand", None, "tp"), P("cand", "tp", None))
    return jax.shard_map(shards, mesh=mesh, in_specs=in_specs, out_specs=out_specs, check_vma=False)
```

```python
import functools

import jax
import jax.numpy as jnp
from jax import lax
from jax.experimental import pallas as pl
from jax.experimental.pallas import tpu as pltpu
from jax.sharding import PartitionSpec as P

D = 4096
HEADS = 32
KV_HEADS = 8
HEAD_DIM = 128
CAND_DEV = 768
LANES = 128
EPSILON = 1e-05
BF = jnp.bfloat16
F32 = jnp.float32

VMEM = pl.BlockSpec(memory_space=pltpu.VMEM)
CORE_PAIRS = [(i, i ^ 1) for i in range(16)]
ACROSS_Z = [(i, i ^ 4) for i in range(8)]
SAME_Z = [[0, 1, 2, 3], [4, 5, 6, 7]]
SAME_CORE_ALL = [[c * 16 + t for c in range(8) for t in range(core, 16, 2)] for core in range(2)]
SAME_CORE = [list(range(core, 16, 2)) for core in range(2)]


def exchange(blocks, axis, groups=None):
    return lax.all_to_all(blocks, axis, 0, 0, axis_index_groups=groups)


def lanes_of(column):
    high = column.astype(BF).astype(F32)
    lane = lax.broadcasted_iota(jnp.int32, (column.shape[0], LANES), 1)
    return jnp.where(lane == 0, high, jnp.where(lane == 1, column - high, 0.0)).astype(BF)


def column_of(lanes):
    return lanes[:, 0:1].astype(F32) + lanes[:, 1:2].astype(F32)


def params(limit_mib):
    return pltpu.CompilerParams(
        dimension_semantics=("arbitrary",), vmem_limit_bytes=limit_mib << 20
    )


def cost(flops, bytes_accessed, transcendentals=0):
    return pl.CostEstimate(
        flops=flops, bytes_accessed=bytes_accessed, transcendentals=transcendentals
    )


def project_kernel(scalars, rows, gain, *refs):
    *weights, out, scaled_out = refs
    wide = rows[...].astype(F32)
    scaled = (wide * gain[...]).astype(BF)
    scaled_out[...] = scaled
    at = 0
    for weight in weights:
        width = weight.shape[1]
        out[:, at : at + width] = jnp.dot(
            scaled, weight[...], preferred_element_type=F32
        ).astype(BF)
        at += width
    out[:, at:] = lanes_of(jnp.sum(wide * wide, axis=1, keepdims=True))


def project(rows, gain, weights, widths, columns, limit_mib, name):
    count, depth = rows.shape
    out_width = sum(widths) + LANES
    tile = count // 2

    def weight_spec(i, width):
        return pl.BlockSpec((depth, width), lambda r, scalars: (0, scalars[i]))

    return pl.pallas_call(
        project_kernel,
        out_shape=[
            jax.ShapeDtypeStruct((count, out_width), BF),
            jax.ShapeDtypeStruct((count, depth), BF),
        ],
        grid_spec=pltpu.PrefetchScalarGridSpec(
            num_scalar_prefetch=1,
            grid=(2,),
            in_specs=[
                pl.BlockSpec((tile, depth), lambda r, scalars: (r, 0)),
                pl.BlockSpec((1, depth), lambda r, scalars: (0, 0)),
            ]
            + [weight_spec(i, width) for i, width in enumerate(widths)],
            out_specs=[
                pl.BlockSpec((tile, out_width), lambda r, scalars: (r, 0)),
                pl.BlockSpec((tile, depth), lambda r, scalars: (r, 0)),
            ],
        ),
        compiler_params=params(limit_mib),
        cost_estimate=cost(2 * count * depth * out_width, 2 * out_width * (count + depth)),
        name=name,
    )(jnp.stack(columns).astype(jnp.int32), rows, gain.reshape(1, depth), *weights)


def copies_kernel(body, scalars, *refs):
    *ins, out = refs
    value = body(*ins)
    for i in range(out.shape[0]):
        out[i] = value


def summed_copies(body, ins, in_specs, scalars, copies, rows, width, name):
    return pl.pallas_call(
        functools.partial(copies_kernel, body),
        out_shape=jax.ShapeDtypeStruct((copies, rows, width), BF),
        grid_spec=pltpu.PrefetchScalarGridSpec(
            num_scalar_prefetch=1,
            grid=(1,),
            in_specs=in_specs,
            out_specs=pl.BlockSpec((copies, rows, width), lambda i, scalars: (0, 0, 0)),
        ),
        compiler_params=params(12),
        cost_estimate=cost(0, 4 * copies * rows * width),
        name=name,
    )(scalars, *ins)


def whole(array):
    return pl.BlockSpec(array.shape, lambda i, scalars: (0,) * array.ndim)


def to_vmem_kernel(blocks, out):
    out[pl.program_id(0)] = blocks[0]


def to_vmem(blocks):
    return pl.pallas_call(
        to_vmem_kernel,
        out_shape=jax.ShapeDtypeStruct(blocks.shape, blocks.dtype),
        grid=(blocks.shape[0],),
        in_specs=[pl.BlockSpec((1,) + blocks.shape[1:], lambda i: (i, 0, 0))],
        out_specs=VMEM,
        compiler_params=params(8),
        cost_estimate=cost(0, 4 * blocks.size),
        name="to_vmem",
    )(blocks)


def qkv_body(received):
    total = jnp.sum(received[...].astype(F32), axis=0)
    width = total.shape[1] - LANES
    squares = total[:, width : width + 1] + total[:, width + 1 : width + 2]
    return (total[:, :width] * lax.rsqrt(squares / D + EPSILON)).astype(BF)


def residual_body(received, rows):
    return (rows[...].astype(F32) + jnp.sum(received[...].astype(F32), axis=0)).astype(BF)


def put_tiles(out, parts):
    at = 0
    for part in parts:
        count = part.shape[0]
        for lane in range(0, part.shape[1], LANES):
            out[at : at + count, :] = part[:, lane : lane + LANES]
            at += count


def sums_kernel(received, res_half, res_across, res_tiles, sums, minus_hidden):
    ff_dev = minus_hidden.shape[1]
    total = jnp.sum(received[...].astype(F32), axis=0)
    squares = total[:, 2 * ff_dev : 2 * ff_dev + 1] + total[:, 2 * ff_dev + 1 : 2 * ff_dev + 2]
    scale = lax.rsqrt(squares / D + EPSILON)
    gate = total[:, :ff_dev] * scale
    up = total[:, ff_dev : 2 * ff_dev] * scale
    hidden = (-(gate * jax.nn.sigmoid(gate) * up)).astype(BF)
    minus_hidden[...] = hidden
    slots = [part[:, :CAND_DEV].astype(BF) for part in (gate, up)]
    put_tiles(sums, slots + [lanes_of(scale), hidden[:, CAND_DEV:]])
    put_tiles(res_tiles, (res_half, res_across))


def gate_up_sums(received, res_half, res_across):
    _, rows, width = received.shape
    ff_dev = (width - LANES) // 2
    half, depth = res_half.shape
    return pl.pallas_call(
        sums_kernel,
        out_shape=[
            jax.ShapeDtypeStruct((2 * half * (depth // LANES), LANES), BF),
            jax.ShapeDtypeStruct((rows * SUMS_TILES, LANES), BF),
            jax.ShapeDtypeStruct((rows, ff_dev), BF),
        ],
        compiler_params=pltpu.CompilerParams(vmem_limit_bytes=14 << 20),
        cost_estimate=cost(0, 4 * received.size, rows * ff_dev),
        name="gate_up_sums",
    )(received, res_half, res_across)


LIVE_AT, LIVES_AT, Z_AT = 1, 2, 10
SUMS_TILES = 2 * CAND_DEV // LANES + 2


def tiles_of(block, first, count, rows):
    tiles = [block[..., first + i * rows : first + (i + 1) * rows, :] for i in range(count)]
    return jnp.concatenate([tile.reshape(-1, LANES) for tile in tiles], axis=1)


def dropped_kernel(flip, scalars, own, across, down, out, rows):
    cands, blocks, chunks, chunk, width = out.shape
    own_first = scalars[Z_AT] == 0
    unit = lax.broadcasted_iota(jnp.int32, own.shape, 1)
    count = own.shape[0]
    tiles = CAND_DEV // LANES
    gate = tiles_of(across[...], 0, tiles, count).astype(F32)
    up = tiles_of(across[...], tiles * count, tiles, count).astype(F32)
    rest = tiles_of(across[...], (2 * tiles + 1) * count, 1, count).astype(F32)
    here = own[...].astype(F32)
    there = jnp.concatenate([-(gate * jax.nn.sigmoid(gate) * up), rest], axis=1)
    for z in range(2):
        values = jnp.where(own_first == (z == 0), here, there)
        for c in range(cands):
            dropped = jnp.where(unit >= scalars[LIVES_AT + c], values, 0.0).astype(BF)
            rows[(2 * c + z) * count : (2 * c + z + 1) * count, :] = dropped
    core = 1 - scalars[0] if flip else scalars[0]
    for i in range(blocks):
        total = jnp.dot(rows[...], down[blocks * core + i], preferred_element_type=F32)
        out[:, i] = total.astype(BF).reshape(cands, chunks, chunk, width)


def dropped_output(scalars, own, across, down_four, flip):
    tok_cand, ff_dev = own.shape
    width = down_four.shape[2]
    return pl.pallas_call(
        functools.partial(dropped_kernel, flip),
        out_shape=jax.ShapeDtypeStruct((8, 2, 4, tok_cand // 2, width), BF),
        in_specs=[pl.BlockSpec(memory_space=pltpu.SMEM), VMEM, VMEM, VMEM],
        out_specs=VMEM,
        scratch_shapes=[pltpu.VMEM((16 * tok_cand, ff_dev), BF)],
        compiler_params=pltpu.CompilerParams(vmem_limit_bytes=11 << 20),
        cost_estimate=cost(64 * tok_cand * ff_dev * width, 8 * (ff_dev + 8 * tok_cand) * width),
        name="dropped_output",
    )(scalars, own, across, down_four)


def factors_kernel(rows, scalars, own_sums, across_sums, gate_factor, up_factor, used_t):
    own_z = (scalars[0] + pl.program_id(0)) % 2 == scalars[Z_AT]
    payload = jnp.where(own_z, own_sums[...].astype(F32), across_sums[...].astype(F32))
    tiles = CAND_DEV // LANES
    gate = tiles_of(payload, 0, tiles, rows)
    up = tiles_of(payload, tiles * rows, tiles, rows)
    keep = lax.broadcasted_iota(jnp.int32, gate.shape, 1) < scalars[LIVE_AT]
    scale = jnp.where(keep, column_of(tiles_of(payload, 2 * tiles * rows, 1, rows)), 0.0)
    sigmoid = jax.nn.sigmoid(gate)
    activated = gate * sigmoid
    slope = sigmoid * (1.0 + gate * (1.0 - sigmoid))
    at = pl.program_id(0)
    half = gate.shape[0]
    gate_factor[pl.ds(at * half, half), :] = (up * slope * scale).astype(BF)
    up_factor[pl.ds(at * half, half), :] = (activated * scale).astype(BF)
    turned = jnp.where(keep, activated * up, 0.0).T.astype(BF)
    used_t[:, pl.ds(pl.multiple_of(at * half, half), half)] = turned


def factors(scalars, own_sums, across_sums, rows):
    groups = own_sums.shape[0]
    half = groups * rows
    tok_count = 2 * half
    factor = jax.ShapeDtypeStruct((tok_count, CAND_DEV), BF)
    return pl.pallas_call(
        functools.partial(factors_kernel, rows),
        out_shape=[factor, factor, jax.ShapeDtypeStruct((CAND_DEV, tok_count), BF)],
        grid_spec=pltpu.PrefetchScalarGridSpec(
            num_scalar_prefetch=1,
            grid=(2,),
            in_specs=[
                pl.BlockSpec((groups, rows * SUMS_TILES, LANES), lambda i, scalars: (0, 0, 0)),
            ]
            + [
                pl.BlockSpec((groups, rows * SUMS_TILES, LANES), lambda i, scalars: (0, 0, 0)),
            ],
            out_specs=[VMEM] * 3,
        ),
        compiler_params=params(24),
        cost_estimate=cost(0, 14 * tok_count * CAND_DEV, tok_count * CAND_DEV),
        name="factors",
    )(scalars, own_sums, across_sums)


def sum_error_kernel(received, out):
    value = jnp.sum(received[...].astype(F32), axis=1).astype(BF)
    for i in range(out.shape[0]):
        out[i] = value


def sum_error(received):
    groups, chips, rows, width = received.shape
    return pl.pallas_call(
        sum_error_kernel,
        out_shape=jax.ShapeDtypeStruct((chips, groups, rows, width), BF),
        grid=(4,),
        in_specs=[pl.BlockSpec((groups // 4, chips, rows, width), lambda i: (i, 0, 0, 0))],
        out_specs=pl.BlockSpec((chips, groups // 4, rows, width), lambda i: (0, i, 0, 0)),
        compiler_params=params(12),
        cost_estimate=cost(0, 4 * received.size),
        name="sum_error",
    )(received)


def contract(left, right, left_dim, right_dim):
    return lax.dot_general(
        left, right, (((left_dim,), (right_dim,)), ((), ())), preferred_element_type=F32
    )


def grad_rows_of(scalars, grad, block, z):
    rows = []
    for half in (scalars[0], 1 - scalars[0]):
        for y in range(grad.shape[3]):
            rows += [grad[block, 2 * half + i, z, y] for i in range(2)]
    return jnp.concatenate(rows, axis=0)


def back_product(scalars, grad, own_four, across_four, core):
    total = None
    for z, down in ((scalars[Z_AT], own_four), (1 - scalars[Z_AT], across_four)):
        rows = [grad_rows_of(scalars, grad, block, z) for block in range(2)]
        units = [down[2 * core + block, :CAND_DEV] for block in range(2)]
        product = contract(jnp.concatenate(rows, axis=1), jnp.concatenate(units, axis=1), 1, 1)
        total = product if total is None else total + product
    return total


def back_kernel(scalars, grad, own_four, across_four, out):
    out[...] = back_product(scalars, grad, own_four, across_four, scalars[0])


def own_back(scalars, grad_own, own_four, across_four):
    _, chunks, z, y, rows, width = grad_own.shape
    tok_count = chunks * y * rows
    return pl.pallas_call(
        back_kernel,
        out_shape=jax.ShapeDtypeStruct((tok_count, CAND_DEV), F32),
        in_specs=[pl.BlockSpec(memory_space=pltpu.SMEM), VMEM, VMEM, VMEM],
        out_specs=VMEM,
        compiler_params=pltpu.CompilerParams(vmem_limit_bytes=12 << 20),
        cost_estimate=cost(8 * tok_count * width * CAND_DEV, 10 << 20),
        name="own_back",
    )(scalars, grad_own, own_four, across_four)


def gradient_kernel(
    scalars,
    res_1,
    res_2,
    own,
    other,
    own_four,
    across_four,
    start,
    gate_factor,
    up_factor,
    used_t,
    gate_out,
    up_out,
    down_out,
    terms,
):
    step = pl.program_id(0)

    @pl.when(step == 0)
    def _():
        total = start[...] + back_product(scalars, other, own_four, across_four, 1 - scalars[0])
        terms[:, :CAND_DEV] = (total * gate_factor[...].astype(F32)).astype(BF)
        terms[:, CAND_DEV:] = (total * up_factor[...].astype(F32)).astype(BF)

    for at, grad in enumerate((own, other)):

        @pl.when((step >= 1) & (step < 5) & ((step - 1) // 2 == at))
        def _(grad=grad):
            z = (step - 1) % 2
            rows = [grad_rows_of(scalars, grad, block, z) for block in range(2)]
            rows = jnp.concatenate(rows, axis=1)
            down_out[0] = jnp.dot(used_t[...], rows, preferred_element_type=F32).astype(BF)

    @pl.when(step >= 5)
    def _():
        tok_count, width = terms.shape[0], gate_out.shape[1]
        half, tiles = tok_count // 2, width // LANES
        at = pl.multiple_of((step - 5) % 2 * half * tiles, half * tiles)
        res = [
            tiles_of(ref[0, pl.ds(at, half * tiles), :], 0, tiles, half) for ref in (res_1, res_2)
        ]
        both = contract(jnp.concatenate(res, axis=0), terms[...], 0, 0).astype(BF)
        gate_out[0] = both[:, :CAND_DEV]
        up_out[0] = both[:, CAND_DEV:]


def gradients(
    scalars, gathered, gathered_other, grad_own, grad_other, own_four, across_four, start, *factor
):
    tok_count, width = start.shape[0], own_four.shape[2]
    groups = 2 * own_four.shape[0]

    def late_pair(i, scalars):
        at = jnp.clip(i - 1, 0, 3)
        return at % 2 * 2 + jnp.where(at < 2, scalars[0], 1 - scalars[0])

    out = jax.ShapeDtypeStruct((1, groups * width, CAND_DEV), BF)

    def late(i, scalars):
        at = jnp.maximum(i - 5, 0)
        return 4 * ((scalars[Z_AT] + at) % 2) + at // 2

    out_spec = pl.BlockSpec((1, width, CAND_DEV), lambda i, scalars: (0, late(i, scalars), 0))
    res_spec = pl.BlockSpec(
        (1, tok_count * width // LANES, LANES),
        lambda i, scalars: (jnp.maximum(i - 5, 0) // 2, 0, 0),
    )
    product = 2 * tok_count * groups * width * CAND_DEV
    return pl.pallas_call(
        gradient_kernel,
        out_shape=[out, out, jax.ShapeDtypeStruct((1, CAND_DEV, groups * width), BF)],
        grid_spec=pltpu.PrefetchScalarGridSpec(
            num_scalar_prefetch=1,
            grid=(5 + groups,),
            in_specs=[res_spec, res_spec] + [VMEM] * 8,
            out_specs=[
                out_spec,
                out_spec,
                pl.BlockSpec(
                    (1, CAND_DEV, 2 * width), lambda i, scalars: (0, 0, late_pair(i, scalars))
                ),
            ],
            scratch_shapes=[pltpu.VMEM((tok_count, 2 * CAND_DEV), BF)],
        ),
        compiler_params=params(20),
        cost_estimate=cost(7 * product // 2, 40 << 20),
        name="gradients",
    )(
        scalars,
        gathered,
        gathered_other,
        grad_own,
        grad_other,
        own_four,
        across_four,
        start,
        *factor,
    )


def shards(
    tokens,
    attn_gain,
    ffn_gain,
    w_query,
    w_key,
    w_value,
    w_out,
    w_gate,
    w_up,
    w_down,
    doc_ids,
    widths,
):
    cand_index = lax.axis_index("cand")
    tp_index = lax.axis_index("tp")
    core = (tp_index % 2).astype(jnp.int32)
    cands = lax.axis_size("cand")
    tps = lax.axis_size("tp")
    tok_count, width = tokens.shape
    ff_dev = w_gate.shape[1]
    tok_cand = tok_count // cands
    tok_tp = tok_count // tps
    nothing = jnp.zeros((1,), jnp.int32)

    heads_dev = w_query.shape[1] // HEAD_DIM
    kv_index = tp_index * heads_dev // (HEADS // KV_HEADS)
    zero = jnp.zeros_like(kv_index)
    q_width = heads_dev * HEAD_DIM
    part, _ = project(
        tokens,
        attn_gain,
        (w_query, w_key, w_value),
        (q_width, HEAD_DIM, HEAD_DIM),
        (zero, kv_index, kv_index),
        60,
        "project_qkv",
    )
    received = exchange(part.reshape(cands, tok_cand, part.shape[1]), "cand")
    received, w_down = lax.optimization_barrier((received, w_down))
    own_four = lax.all_gather(w_down, "cand", axis=0, axis_index_groups=SAME_Z)
    down_across = lax.ppermute(w_down[:CAND_DEV], "cand", ACROSS_Z)
    qkv_width = part.shape[1] - LANES
    copies = summed_copies(
        qkv_body, (received,), [whole(received)], nothing, cands, tok_cand, qkv_width, "sum_qkv"
    )
    qkv = exchange(copies, "cand").reshape(tok_count, qkv_width)
    query = qkv[:, :q_width].reshape(tok_count, heads_dev, HEAD_DIM)
    key_rows = qkv[:, q_width : q_width + HEAD_DIM]
    value_rows = qkv[:, q_width + HEAD_DIM :]

    scores = jnp.einsum(
        "qhd,kd->hqk", query, key_rows, preferred_element_type=F32
    ) * HEAD_DIM ** (-0.5)
    position = lax.iota(jnp.int32, tok_count)
    allowed = (position[None, :] <= position[:, None]) & (doc_ids[None, :] == doc_ids[:, None])
    scores = jnp.where(allowed[None], scores, -1e30)
    peak_score = jnp.max(scores, axis=-1, keepdims=True)
    expo = jnp.exp(scores - peak_score)
    weights_bf = (expo / jnp.sum(expo, axis=-1, keepdims=True)).astype(BF)
    attended = jnp.einsum("hqk,kd->qhd", weights_bf, value_rows, preferred_element_type=F32)
    attended = attended.astype(BF).reshape(tok_count, heads_dev * HEAD_DIM)
    out_part = jnp.dot(attended, w_out, preferred_element_type=F32).astype(BF)
    received = exchange(out_part.reshape(tps, tok_tp, width), "tp")
    received, down_across = lax.optimization_barrier((received, down_across))
    copies = summed_copies(
        residual_body,
        (received, tokens),
        [
            whole(received),
            pl.BlockSpec((tok_tp, width), lambda i, scalars: (scalars[0], 0)),
        ],
        tp_index.astype(jnp.int32)[None],
        tps,
        tok_tp,
        width,
        "sum_attention",
    )
    residual = exchange(copies, "tp").reshape(tok_count, width)

    residual, own_four = lax.optimization_barrier((residual, own_four))
    own_four = to_vmem(own_four)
    part, scaled_res = project(
        residual, ffn_gain, (w_gate, w_up), (ff_dev, ff_dev), (zero, zero), 16, "project_gate_up"
    )
    tok_half = tok_count // 2
    scaled_res, down_across = lax.optimization_barrier((scaled_res, down_across))
    across_four = lax.all_gather(down_across, "cand", axis=0, axis_index_groups=SAME_Z)
    res_half = lax.dynamic_slice_in_dim(scaled_res, core * tok_half, tok_half, 0)
    res_across = lax.ppermute(res_half, "cand", ACROSS_Z)
    received = exchange(part.reshape(cands, tok_cand, part.shape[1]), "cand")
    received, own_four, res_across = lax.optimization_barrier((received, own_four, res_across))
    res_tiles, sums, minus_hidden = gate_up_sums(received, res_half, res_across)
    sums_across = lax.ppermute(sums, "cand", ACROSS_Z)

    live = (widths // tps).astype(jnp.int32)
    own_live = jnp.sum(jnp.where(lax.iota(jnp.int32, widths.shape[0]) == cand_index, live, 0))
    z_index = (cand_index // 4).astype(jnp.int32)
    scalars = jnp.concatenate([core[None], own_live[None], live, z_index[None]])
    sent = dropped_output(scalars, minus_hidden, sums_across, own_four, True)
    away = lax.ppermute(sent, "tp", CORE_PAIRS)
    kept = dropped_output(scalars, minus_hidden, sums_across, own_four, False)
    parts = (kept.astype(F32) + away.astype(F32)).astype(BF)
    payload = jnp.concatenate([res_tiles, sums, sums_across], axis=0)
    payload, across_four = lax.optimization_barrier((payload, across_four))
    gathered = lax.all_gather(payload, "cand", axis=0, axis_index_groups=SAME_Z)
    chunk = tok_cand // 2
    parts = parts.reshape(cands * tps // 2, chunk, width)
    received = exchange(parts, ("cand", "tp"), SAME_CORE_ALL)
    copies = sum_error(received.reshape(cands, tps // 2, chunk, width))
    gathered_other = lax.ppermute(gathered, "tp", CORE_PAIRS)
    grad_own = exchange(copies, "tp", SAME_CORE).reshape(2, 4, 2, 4, chunk, width)

    factor = factors(
        scalars,
        gathered[:, -2 * sums.shape[0] : -sums.shape[0]],
        gathered[:, -sums.shape[0] :],
        tok_cand,
    )
    across_four = to_vmem(across_four)
    grad_own, across_four, *factor = lax.optimization_barrier((grad_own, across_four, *factor))
    grad_other = lax.ppermute(grad_own, "tp", CORE_PAIRS)
    start = own_back(scalars, grad_own, own_four, across_four)
    return tuple(
        gradients(
            scalars, gathered, gathered_other, grad_own, grad_other, own_four, across_four, start, *factor
        )
    )


def solution(mesh):
    in_specs = (
        P(None, "cand"),
        P("cand"),
        P("cand"),
        P("cand", "tp"),
        P("cand", None),
        P("cand", None),
        P("tp", "cand"),
        P("cand", "tp"),
        P("cand", "tp"),
        P("tp", "cand"),
        P(),
        P(),
    )
    out_specs = (P("cand", None, "tp"), P("cand", None, "tp"), P("cand", "tp", None))
    return jax.shard_map(shards, mesh=mesh, in_specs=in_specs, out_specs=out_specs, check_vma=False)
```

```python
import functools

import jax
import jax.numpy as jnp
from jax import lax
from jax.experimental import pallas as pl
from jax.experimental.pallas import tpu as pltpu
from jax.sharding import PartitionSpec as P

D = 4096
HEADS = 32
KV_HEADS = 8
HEAD_DIM = 128
CAND_DEV = 768
LANES = 128
EPSILON = 1e-05
BF = jnp.bfloat16
F32 = jnp.float32

VMEM = pl.BlockSpec(memory_space=pltpu.VMEM)
CORE_PAIRS = [(i, i ^ 1) for i in range(16)]
ACROSS_Z = [(i, i ^ 4) for i in range(8)]
SAME_Z = [[0, 1, 2, 3], [4, 5, 6, 7]]
SAME_CORE_ALL = [[c * 16 + t for c in range(8) for t in range(core, 16, 2)] for core in range(2)]
SAME_CORE = [list(range(core, 16, 2)) for core in range(2)]


def exchange(blocks, axis, groups=None):
    return lax.all_to_all(blocks, axis, 0, 0, axis_index_groups=groups)


def lanes_of(column):
    high = column.astype(BF).astype(F32)
    lane = lax.broadcasted_iota(jnp.int32, (column.shape[0], LANES), 1)
    return jnp.where(lane == 0, high, jnp.where(lane == 1, column - high, 0.0)).astype(BF)


def column_of(lanes):
    return lanes[:, 0:1].astype(F32) + lanes[:, 1:2].astype(F32)


def params(limit_mib):
    return pltpu.CompilerParams(
        dimension_semantics=("arbitrary",), vmem_limit_bytes=limit_mib << 20
    )


def cost(flops, bytes_accessed, transcendentals=0):
    return pl.CostEstimate(
        flops=flops, bytes_accessed=bytes_accessed, transcendentals=transcendentals
    )


def project_kernel(scalars, rows, gain, *refs):
    *weights, out, scaled_out = refs
    wide = rows[...].astype(F32)
    scaled = (wide * gain[...]).astype(BF)
    scaled_out[...] = scaled
    at = 0
    for weight in weights:
        width = weight.shape[1]
        out[:, at : at + width] = jnp.dot(
            scaled, weight[...], preferred_element_type=F32
        ).astype(BF)
        at += width
    out[:, at:] = lanes_of(jnp.sum(wide * wide, axis=1, keepdims=True))


def project(rows, gain, weights, widths, columns, limit_mib, name):
    count, depth = rows.shape
    out_width = sum(widths) + LANES
    tile = count // 2

    def weight_spec(i, width):
        return pl.BlockSpec((depth, width), lambda r, scalars: (0, scalars[i]))

    return pl.pallas_call(
        project_kernel,
        out_shape=[
            jax.ShapeDtypeStruct((count, out_width), BF),
            jax.ShapeDtypeStruct((count, depth), BF),
        ],
        grid_spec=pltpu.PrefetchScalarGridSpec(
            num_scalar_prefetch=1,
            grid=(2,),
            in_specs=[
                pl.BlockSpec((tile, depth), lambda r, scalars: (r, 0)),
                pl.BlockSpec((1, depth), lambda r, scalars: (0, 0)),
            ]
            + [weight_spec(i, width) for i, width in enumerate(widths)],
            out_specs=[
                pl.BlockSpec((tile, out_width), lambda r, scalars: (r, 0)),
                pl.BlockSpec((tile, depth), lambda r, scalars: (r, 0)),
            ],
        ),
        compiler_params=params(limit_mib),
        cost_estimate=cost(2 * count * depth * out_width, 2 * out_width * (count + depth)),
        name=name,
    )(jnp.stack(columns).astype(jnp.int32), rows, gain.reshape(1, depth), *weights)


def copies_kernel(body, scalars, *refs):
    *ins, out = refs
    value = body(*ins)
    for i in range(out.shape[0]):
        out[i] = value


def summed_copies(body, ins, in_specs, scalars, copies, rows, width, name):
    return pl.pallas_call(
        functools.partial(copies_kernel, body),
        out_shape=jax.ShapeDtypeStruct((copies, rows, width), BF),
        grid_spec=pltpu.PrefetchScalarGridSpec(
            num_scalar_prefetch=1,
            grid=(1,),
            in_specs=in_specs,
            out_specs=pl.BlockSpec((copies, rows, width), lambda i, scalars: (0, 0, 0)),
        ),
        compiler_params=params(12),
        cost_estimate=cost(0, 4 * copies * rows * width),
        name=name,
    )(scalars, *ins)


def whole(array):
    return pl.BlockSpec(array.shape, lambda i, scalars: (0,) * array.ndim)


def to_vmem_kernel(blocks, out):
    out[pl.program_id(0)] = blocks[0]


def to_vmem(blocks):
    return pl.pallas_call(
        to_vmem_kernel,
        out_shape=jax.ShapeDtypeStruct(blocks.shape, blocks.dtype),
        grid=(blocks.shape[0],),
        in_specs=[pl.BlockSpec((1,) + blocks.shape[1:], lambda i: (i, 0, 0))],
        out_specs=VMEM,
        compiler_params=params(8),
        cost_estimate=cost(0, 4 * blocks.size),
        name="to_vmem",
    )(blocks)


def qkv_body(received):
    total = jnp.sum(received[...].astype(F32), axis=0)
    width = total.shape[1] - LANES
    squares = total[:, width : width + 1] + total[:, width + 1 : width + 2]
    return (total[:, :width] * lax.rsqrt(squares / D + EPSILON)).astype(BF)


def residual_body(received, rows):
    return (rows[...].astype(F32) + jnp.sum(received[...].astype(F32), axis=0)).astype(BF)


def put_tiles(out, parts):
    at = 0
    for part in parts:
        count = part.shape[0]
        for lane in range(0, part.shape[1], LANES):
            out[at : at + count, :] = part[:, lane : lane + LANES]
            at += count


def sums_kernel(received, res_half, res_across, res_tiles, sums, minus_hidden):
    ff_dev = minus_hidden.shape[1]
    total = jnp.sum(received[...].astype(F32), axis=0)
    squares = total[:, 2 * ff_dev : 2 * ff_dev + 1] + total[:, 2 * ff_dev + 1 : 2 * ff_dev + 2]
    scale = lax.rsqrt(squares / D + EPSILON)
    gate = total[:, :ff_dev] * scale
    up = total[:, ff_dev : 2 * ff_dev] * scale
    hidden = (-(gate * jax.nn.sigmoid(gate) * up)).astype(BF)
    minus_hidden[...] = hidden
    slots = [part[:, :CAND_DEV].astype(BF) for part in (gate, up)]
    put_tiles(sums, slots + [lanes_of(scale), hidden[:, CAND_DEV:]])
    put_tiles(res_tiles, (res_half, res_across))


def gate_up_sums(received, res_half, res_across):
    _, rows, width = received.shape
    ff_dev = (width - LANES) // 2
    half, depth = res_half.shape
    return pl.pallas_call(
        sums_kernel,
        out_shape=[
            jax.ShapeDtypeStruct((2 * half * (depth // LANES), LANES), BF),
            jax.ShapeDtypeStruct((rows * SUMS_TILES, LANES), BF),
            jax.ShapeDtypeStruct((rows, ff_dev), BF),
        ],
        compiler_params=pltpu.CompilerParams(vmem_limit_bytes=14 << 20),
        cost_estimate=cost(0, 4 * received.size, rows * ff_dev),
        name="gate_up_sums",
    )(received, res_half, res_across)


LIVE_AT, LIVES_AT, Z_AT = 1, 2, 10
SUMS_TILES = 2 * CAND_DEV // LANES + 2


def tiles_of(block, first, count, rows):
    tiles = [block[..., first + i * rows : first + (i + 1) * rows, :] for i in range(count)]
    return jnp.concatenate([tile.reshape(-1, LANES) for tile in tiles], axis=1)


def dropped_kernel(flip, scalars, own, across, down, out, rows):
    cands, blocks, chunks, chunk, width = out.shape
    own_first = scalars[Z_AT] == 0
    unit = lax.broadcasted_iota(jnp.int32, own.shape, 1)
    count = own.shape[0]
    tiles = CAND_DEV // LANES
    gate = tiles_of(across[...], 0, tiles, count).astype(F32)
    up = tiles_of(across[...], tiles * count, tiles, count).astype(F32)
    rest = tiles_of(across[...], (2 * tiles + 1) * count, 1, count).astype(F32)
    here = own[...].astype(F32)
    there = jnp.concatenate([-(gate * jax.nn.sigmoid(gate) * up), rest], axis=1)
    for z in range(2):
        values = jnp.where(own_first == (z == 0), here, there)
        for c in range(cands):
            dropped = jnp.where(unit >= scalars[LIVES_AT + c], values, 0.0).astype(BF)
            rows[(2 * c + z) * count : (2 * c + z + 1) * count, :] = dropped
    core = 1 - scalars[0] if flip else scalars[0]
    for i in range(blocks):
        total = jnp.dot(rows[...], down[blocks * core + i], preferred_element_type=F32)
        out[:, i] = total.astype(BF).reshape(cands, chunks, chunk, width)


def dropped_output(scalars, own, across, down_four, flip):
    tok_cand, ff_dev = own.shape
    width = down_four.shape[2]
    return pl.pallas_call(
        functools.partial(dropped_kernel, flip),
        out_shape=jax.ShapeDtypeStruct((8, 2, 4, tok_cand // 2, width), BF),
        in_specs=[pl.BlockSpec(memory_space=pltpu.SMEM), VMEM, VMEM, VMEM],
        out_specs=VMEM,
        scratch_shapes=[pltpu.VMEM((16 * tok_cand, ff_dev), BF)],
        compiler_params=pltpu.CompilerParams(vmem_limit_bytes=11 << 20),
        cost_estimate=cost(64 * tok_cand * ff_dev * width, 8 * (ff_dev + 8 * tok_cand) * width),
        name="dropped_output",
    )(scalars, own, across, down_four)


def factors_kernel(rows, scalars, own_sums, across_sums, gate_factor, up_factor, used_t):
    own_z = (scalars[0] + pl.program_id(0)) % 2 == scalars[Z_AT]
    payload = jnp.where(own_z, own_sums[...].astype(F32), across_sums[...].astype(F32))
    tiles = CAND_DEV // LANES
    gate = tiles_of(payload, 0, tiles, rows)
    up = tiles_of(payload, tiles * rows, tiles, rows)
    keep = lax.broadcasted_iota(jnp.int32, gate.shape, 1) < scalars[LIVE_AT]
    scale = jnp.where(keep, column_of(tiles_of(payload, 2 * tiles * rows, 1, rows)), 0.0)
    sigmoid = jax.nn.sigmoid(gate)
    activated = gate * sigmoid
    slope = sigmoid * (1.0 + gate * (1.0 - sigmoid))
    at = pl.program_id(0)
    half = gate.shape[0]
    gate_factor[pl.ds(at * half, half), :] = (up * slope * scale).astype(BF)
    up_factor[pl.ds(at * half, half), :] = (activated * scale).astype(BF)
    turned = jnp.where(keep, activated * up, 0.0).T.astype(BF)
    used_t[:, pl.ds(pl.multiple_of(at * half, half), half)] = turned


def factors(scalars, own_sums, across_sums, rows):
    groups = own_sums.shape[0]
    half = groups * rows
    tok_count = 2 * half
    factor = jax.ShapeDtypeStruct((tok_count, CAND_DEV), BF)
    return pl.pallas_call(
        functools.partial(factors_kernel, rows),
        out_shape=[factor, factor, jax.ShapeDtypeStruct((CAND_DEV, tok_count), BF)],
        grid_spec=pltpu.PrefetchScalarGridSpec(
            num_scalar_prefetch=1,
            grid=(2,),
            in_specs=[
                pl.BlockSpec((groups, rows * SUMS_TILES, LANES), lambda i, scalars: (0, 0, 0)),
            ]
            + [
                pl.BlockSpec((groups, rows * SUMS_TILES, LANES), lambda i, scalars: (0, 0, 0)),
            ],
            out_specs=[VMEM] * 3,
        ),
        compiler_params=params(24),
        cost_estimate=cost(0, 14 * tok_count * CAND_DEV, tok_count * CAND_DEV),
        name="factors",
    )(scalars, own_sums, across_sums)


def sum_error_kernel(received, out):
    value = jnp.sum(received[...].astype(F32), axis=1).astype(BF)
    for i in range(out.shape[0]):
        out[i] = value


def sum_error(received):
    groups, chips, rows, width = received.shape
    return pl.pallas_call(
        sum_error_kernel,
        out_shape=jax.ShapeDtypeStruct((chips, groups, rows, width), BF),
        grid=(4,),
        in_specs=[pl.BlockSpec((groups // 4, chips, rows, width), lambda i: (i, 0, 0, 0))],
        out_specs=pl.BlockSpec((chips, groups // 4, rows, width), lambda i: (0, i, 0, 0)),
        compiler_params=params(12),
        cost_estimate=cost(0, 4 * received.size),
        name="sum_error",
    )(received)


def contract(left, right, left_dim, right_dim):
    return lax.dot_general(
        left, right, (((left_dim,), (right_dim,)), ((), ())), preferred_element_type=F32
    )


def grad_rows_of(scalars, grad, block, z):
    rows = []
    for half in (scalars[0], 1 - scalars[0]):
        for y in range(grad.shape[3]):
            rows += [grad[block, 2 * half + i, z, y] for i in range(2)]
    return jnp.concatenate(rows, axis=0)


def back_product(scalars, grad, own_two, across_two):
    total = None
    for z, down in ((scalars[Z_AT], own_two), (1 - scalars[Z_AT], across_two)):
        rows = [grad_rows_of(scalars, grad, block, z) for block in range(2)]
        units = [down[block] for block in range(2)]
        product = contract(jnp.concatenate(rows, axis=1), jnp.concatenate(units, axis=1), 1, 1)
        total = product if total is None else total + product
    return total


def back_kernel(scalars, grad, own_four, across_four, out):
    out[...] = back_product(scalars, grad, own_four, across_four)


def own_back(scalars, grad_own, own_four, across_four):
    _, chunks, z, y, rows, width = grad_own.shape
    tok_count = chunks * y * rows
    return pl.pallas_call(
        back_kernel,
        out_shape=jax.ShapeDtypeStruct((tok_count, CAND_DEV), F32),
        in_specs=[pl.BlockSpec(memory_space=pltpu.SMEM), VMEM, VMEM, VMEM],
        out_specs=VMEM,
        compiler_params=pltpu.CompilerParams(vmem_limit_bytes=12 << 20),
        cost_estimate=cost(8 * tok_count * width * CAND_DEV, 10 << 20),
        name="own_back",
    )(scalars, grad_own, own_four, across_four)


def gradient_kernel(
    scalars,
    res_1,
    res_2,
    own,
    other,
    own_four,
    across_four,
    start,
    gate_factor,
    up_factor,
    used_t,
    gate_out,
    up_out,
    down_out,
    terms,
):
    step = pl.program_id(0)

    @pl.when(step == 0)
    def _():
        total = start[...] + back_product(scalars, other, own_four, across_four)
        terms[:, :CAND_DEV] = (total * gate_factor[...].astype(F32)).astype(BF)
        terms[:, CAND_DEV:] = (total * up_factor[...].astype(F32)).astype(BF)

    for at, grad in enumerate((own, other)):

        @pl.when((step >= 1) & (step < 5) & ((step - 1) // 2 == at))
        def _(grad=grad):
            z = (step - 1) % 2
            rows = [grad_rows_of(scalars, grad, block, z) for block in range(2)]
            rows = jnp.concatenate(rows, axis=1)
            down_out[0] = jnp.dot(used_t[...], rows, preferred_element_type=F32).astype(BF)

    @pl.when(step >= 5)
    def _():
        tok_count, width = terms.shape[0], gate_out.shape[1]
        half, tiles = tok_count // 2, width // LANES
        at = pl.multiple_of((step - 5) % 2 * half * tiles, half * tiles)
        res = [
            tiles_of(ref[0, pl.ds(at, half * tiles), :], 0, tiles, half) for ref in (res_1, res_2)
        ]
        both = contract(jnp.concatenate(res, axis=0), terms[...], 0, 0).astype(BF)
        gate_out[0] = both[:, :CAND_DEV]
        up_out[0] = both[:, CAND_DEV:]


def gradients(
    scalars, gathered, gathered_other, grad_own, grad_other, own_four, across_four, start, *factor
):
    tok_count, width = start.shape[0], own_four.shape[2]
    groups = 4 * own_four.shape[0]

    def late_pair(i, scalars):
        at = jnp.clip(i - 1, 0, 3)
        return at % 2 * 2 + jnp.where(at < 2, scalars[0], 1 - scalars[0])

    out = jax.ShapeDtypeStruct((1, groups * width, CAND_DEV), BF)

    def late(i, scalars):
        at = jnp.maximum(i - 5, 0)
        return 4 * ((scalars[Z_AT] + at) % 2) + at // 2

    out_spec = pl.BlockSpec((1, width, CAND_DEV), lambda i, scalars: (0, late(i, scalars), 0))
    res_spec = pl.BlockSpec(
        (1, tok_count * width // LANES, LANES),
        lambda i, scalars: (jnp.maximum(i - 5, 0) // 2, 0, 0),
    )
    product = 2 * tok_count * groups * width * CAND_DEV
    return pl.pallas_call(
        gradient_kernel,
        out_shape=[out, out, jax.ShapeDtypeStruct((1, CAND_DEV, groups * width), BF)],
        grid_spec=pltpu.PrefetchScalarGridSpec(
            num_scalar_prefetch=1,
            grid=(5 + groups,),
            in_specs=[res_spec, res_spec] + [VMEM] * 8,
            out_specs=[
                out_spec,
                out_spec,
                pl.BlockSpec(
                    (1, CAND_DEV, 2 * width), lambda i, scalars: (0, 0, late_pair(i, scalars))
                ),
            ],
            scratch_shapes=[pltpu.VMEM((tok_count, 2 * CAND_DEV), BF)],
        ),
        compiler_params=params(20),
        cost_estimate=cost(7 * product // 2, 40 << 20),
        name="gradients",
    )(
        scalars,
        gathered,
        gathered_other,
        grad_own,
        grad_other,
        own_four,
        across_four,
        start,
        *factor,
    )


def shards(
    tokens,
    attn_gain,
    ffn_gain,
    w_query,
    w_key,
    w_value,
    w_out,
    w_gate,
    w_up,
    w_down,
    doc_ids,
    widths,
):
    cand_index = lax.axis_index("cand")
    tp_index = lax.axis_index("tp")
    core = (tp_index % 2).astype(jnp.int32)
    cands = lax.axis_size("cand")
    tps = lax.axis_size("tp")
    tok_count, width = tokens.shape
    ff_dev = w_gate.shape[1]
    tok_cand = tok_count // cands
    tok_tp = tok_count // tps
    nothing = jnp.zeros((1,), jnp.int32)

    heads_dev = w_query.shape[1] // HEAD_DIM
    kv_index = tp_index * heads_dev // (HEADS // KV_HEADS)
    zero = jnp.zeros_like(kv_index)
    q_width = heads_dev * HEAD_DIM
    part, _ = project(
        tokens,
        attn_gain,
        (w_query, w_key, w_value),
        (q_width, HEAD_DIM, HEAD_DIM),
        (zero, kv_index, kv_index),
        60,
        "project_qkv",
    )
    received = exchange(part.reshape(cands, tok_cand, part.shape[1]), "cand")
    received, w_down = lax.optimization_barrier((received, w_down))
    own_four = lax.all_gather(w_down, "cand", axis=0, axis_index_groups=SAME_Z)
    down_across = lax.ppermute(w_down[:CAND_DEV], "cand", ACROSS_Z)
    qkv_width = part.shape[1] - LANES
    copies = summed_copies(
        qkv_body, (received,), [whole(received)], nothing, cands, tok_cand, qkv_width, "sum_qkv"
    )
    qkv = exchange(copies, "cand").reshape(tok_count, qkv_width)
    query = qkv[:, :q_width].reshape(tok_count, heads_dev, HEAD_DIM)
    key_rows = qkv[:, q_width : q_width + HEAD_DIM]
    value_rows = qkv[:, q_width + HEAD_DIM :]

    scores = jnp.einsum(
        "qhd,kd->hqk", query, key_rows, preferred_element_type=F32
    ) * HEAD_DIM ** (-0.5)
    position = lax.iota(jnp.int32, tok_count)
    allowed = (position[None, :] <= position[:, None]) & (doc_ids[None, :] == doc_ids[:, None])
    scores = jnp.where(allowed[None], scores, -1e30)
    peak_score = jnp.max(scores, axis=-1, keepdims=True)
    expo = jnp.exp(scores - peak_score)
    weights_bf = (expo / jnp.sum(expo, axis=-1, keepdims=True)).astype(BF)
    attended = jnp.einsum("hqk,kd->qhd", weights_bf, value_rows, preferred_element_type=F32)
    attended = attended.astype(BF).reshape(tok_count, heads_dev * HEAD_DIM)
    out_part = jnp.dot(attended, w_out, preferred_element_type=F32).astype(BF)
    received = exchange(out_part.reshape(tps, tok_tp, width), "tp")
    received, down_across = lax.optimization_barrier((received, down_across))
    copies = summed_copies(
        residual_body,
        (received, tokens),
        [
            whole(received),
            pl.BlockSpec((tok_tp, width), lambda i, scalars: (scalars[0], 0)),
        ],
        tp_index.astype(jnp.int32)[None],
        tps,
        tok_tp,
        width,
        "sum_attention",
    )
    residual = exchange(copies, "tp").reshape(tok_count, width)

    residual, own_four = lax.optimization_barrier((residual, own_four))
    own_four = to_vmem(own_four)
    part, scaled_res = project(
        residual, ffn_gain, (w_gate, w_up), (ff_dev, ff_dev), (zero, zero), 16, "project_gate_up"
    )
    tok_half = tok_count // 2
    scaled_res, down_across = lax.optimization_barrier((scaled_res, down_across))
    across_four = lax.all_gather(down_across, "cand", axis=0, axis_index_groups=SAME_Z)
    res_half = lax.dynamic_slice_in_dim(scaled_res, core * tok_half, tok_half, 0)
    res_across = lax.ppermute(res_half, "cand", ACROSS_Z)
    received = exchange(part.reshape(cands, tok_cand, part.shape[1]), "cand")
    received, own_four, res_across = lax.optimization_barrier((received, own_four, res_across))
    res_tiles, sums, minus_hidden = gate_up_sums(received, res_half, res_across)
    sums_across = lax.ppermute(sums, "cand", ACROSS_Z)

    live = (widths // tps).astype(jnp.int32)
    own_live = jnp.sum(jnp.where(lax.iota(jnp.int32, widths.shape[0]) == cand_index, live, 0))
    z_index = (cand_index // 4).astype(jnp.int32)
    scalars = jnp.concatenate([core[None], own_live[None], live, z_index[None]])
    sent = dropped_output(scalars, minus_hidden, sums_across, own_four, True)
    away = lax.ppermute(sent, "tp", CORE_PAIRS)
    kept = dropped_output(scalars, minus_hidden, sums_across, own_four, False)
    parts = (kept.astype(F32) + away.astype(F32)).astype(BF)
    payload = jnp.concatenate([res_tiles, sums, sums_across], axis=0)
    payload, across_four = lax.optimization_barrier((payload, across_four))
    gathered = lax.all_gather(payload, "cand", axis=0, axis_index_groups=SAME_Z)
    chunk = tok_cand // 2
    parts = parts.reshape(cands * tps // 2, chunk, width)
    received = exchange(parts, ("cand", "tp"), SAME_CORE_ALL)
    copies = sum_error(received.reshape(cands, tps // 2, chunk, width))
    gathered_other = lax.ppermute(gathered, "tp", CORE_PAIRS)
    grad_own = exchange(copies, "tp", SAME_CORE).reshape(2, 4, 2, 4, chunk, width)

    factor = factors(
        scalars,
        gathered[:, -2 * sums.shape[0] : -sums.shape[0]],
        gathered[:, -sums.shape[0] :],
        tok_cand,
    )
    near, far = (
        [
            lax.dynamic_slice(four, (2 * which, 0, 0), (2, CAND_DEV, width))
            for four in (own_four, across_four)
        ]
        for which in (core, 1 - core)
    )
    grad_own, *held = lax.optimization_barrier((grad_own, *near, *far, *factor))
    near, far, factor = held[:2], held[2:4], held[4:]
    grad_other = lax.ppermute(grad_own, "tp", CORE_PAIRS)
    start = own_back(scalars, grad_own, *near)
    return tuple(
        gradients(
            scalars, gathered, gathered_other, grad_own, grad_other, *far, start, *factor
        )
    )


def solution(mesh):
    in_specs = (
        P(None, "cand"),
        P("cand"),
        P("cand"),
        P("cand", "tp"),
        P("cand", None),
        P("cand", None),
        P("tp", "cand"),
        P("cand", "tp"),
        P("cand", "tp"),
        P("tp", "cand"),
        P(),
        P(),
    )
    out_specs = (P("cand", None, "tp"), P("cand", None, "tp"), P("cand", "tp", None))
    return jax.shard_map(shards, mesh=mesh, in_specs=in_specs, out_specs=out_specs, check_vma=False)
```
